32 devices in a mesh: dp: 4 (over x, core), seq: 8 (over z, y).
Axes of the slice: x: 2, y: 2, z: 4, core: 2. Of those that a mesh axis runs over, the one named last changes fastest.
Arguments:
- tokens: bfloat16 [4, 2048, 768], P('dp', 'seq'), may hold values from -6 to 6
- cotangent: bfloat16 [4, 2048, 768], P('dp', 'seq'), may hold values from -6 to 6
- gain_attn: bfloat16 [768], P(('dp', 'seq')), may hold values from 0.5 to 1.5
- query_w: bfloat16 [768, 768], P(('dp', 'seq')), may hold values from -0.0546875 to 0.0546875
- key_w: bfloat16 [768, 768], P(('dp', 'seq')), may hold values from -0.21875 to 0.21875
- value_w: bfloat16 [768, 768], P(('dp', 'seq')), may hold values from -0.21875 to 0.21875
- output_w: bfloat16 [768, 768], P(None, ('dp', 'seq')), may hold values from -1.25 to 1.25
- rel_table: bfloat16 [32, 12], P('seq'), may hold values from -4 to 4
- rel_bucket: int32 [4095], replicated, may hold values from 0 to 31, as said below
- gain_ffn: bfloat16 [768], P(('dp', 'seq')), may hold values from 0.5 to 1.5
- router_w: bfloat16 [768, 4], P(('dp', 'seq')), may hold values from -0.15625 to 0.15625
- routes: int32 [4, 8, 256, 1], P('dp', 'seq'), may hold values from 0 to 3; in each aligned block of 256 rows (0 to 255, 256 to 511, ..., all dimensions but the last counted through in order) at most 128 rows name the same one
- expert_in: bfloat16 [4, 768, 3072], P('dp', None, 'seq'), may hold values from -0.21875 to 0.21875
- expert_out: bfloat16 [4, 768, 3072], P('dp', None, 'seq'), may hold values from -1.75 to 1.75
Outputs:
- mixed: bfloat16 [4, 2048, 768], P('dp', 'seq')
- grad_tokens: float32 [4, 2048, 768], P('dp', 'seq')
- grad_gain_attn: float32 [768], P(('dp', 'seq'))
- grad_query: float32 [768, 768], P(('dp', 'seq'))
- grad_key: float32 [768, 768], P(('dp', 'seq'))
- grad_value: float32 [768, 768], P(('dp', 'seq'))
- grad_output: float32 [768, 768], P(None, ('dp', 'seq'))
- grad_table: float32 [32, 12], P('seq')
- grad_gain_ffn: float32 [768], P(('dp', 'seq'))
- grad_router: float32 [768, 4], P(('dp', 'seq'))
- grad_expert_in: float32 [4, 768, 3072], P('dp', None, 'seq')
- grad_expert_out: float32 [4, 768, 3072], P('dp', None, 'seq')
The draws below stay inside these ranges and needn't reach their ends.
Inputs may be any that keep to these rules, and one draw needn't show every extreme that they name: `routes`: among the 256 tokens of one device no expert is named more than 128 times, a bound that some block reaches. `rel_bucket`: entry r is the bucket of key position minus query position r - 2047; buckets never fall as the distance grows on either side.
All inputs are finite; a program needn't handle non-finite values.
Results may differ from the reference program's by a relative error of at most 0.018.
Values may be sent and summed in bfloat16 or wider, within the bound.
No kernel may reach another device: no remote copies, remote signals or barrier semaphores. Data moves between devices by JAX's collectives and lax.ppermute only.
A program may use at most 256 MiB of HBM per device.

```python
import math
import jax
import jax.numpy as jnp
import numpy as np
from jax import lax

D = 768
HEADS = 12
HEAD_DIM = 64
FF = 3072
BUCKETS = 32
SEQ_LEN = 2048
TOK_DEV = 256
LOCAL = 256
SEQS = 1
BATCH = 4
INNER = 768
EXPERTS = 4
CAP = 128
N_DP = 4
N_SEQ = 8


def draw_rel_bucket(key, part):
    key = jax.random.fold_in(key, 7)
    shuffled = jax.random.permutation(key, SEQ_LEN - 1) + 1
    cut_points = jnp.sort(shuffled[:BUCKETS // 2 - 1])
    offsets = jnp.arange(2 * SEQ_LEN - 1) - (SEQ_LEN - 1)
    magnitude = jnp.abs(offsets)
    levels = jnp.sum((magnitude[:, None] >= cut_points[None, :]).astype(jnp.int32), axis=1)
    side_base = (offsets > 0).astype(jnp.int32) * (BUCKETS // 2)
    return (side_base + levels).astype(jnp.int32)


def block_levels(stream_key, dims, cuts, smallest, high):
    def one(dim, shards_of):
        draws = jax.random.uniform(jax.random.fold_in(jax.random.fold_in(stream_key, 6), dim), (shards_of,), jnp.float32, smallest / len(cuts), high / len(cuts))
        return jnp.repeat(jnp.exp(draws), dims[dim] // shards_of).reshape((-1,) + (1,) * (len(dims) - dim - 1))

    level = one(*cuts[0])
    for cut in cuts[1:]:
        level = level * one(*cut)
    return level


def deal_out(own_key, own, number, rows, number_of, top, reach, lean):
    order = jax.random.permutation(own_key, number_of)
    heavy_load, common = portions_of(number_of, rows * top, reach, lean, True), portions_of(number_of, rows * top, reach, lean, False)
    places = jnp.arange(number_of)

    def named(lengths, rotation):
        used = int((lengths > 0).sum())
        fixed = max(1, used // 4)
        shifted = fixed + (places - fixed + rotation * (used - fixed)) % max(1, number_of - fixed)
        return jnp.zeros((number_of,), jnp.int32).at[order[jnp.where(places < fixed, places, shifted)]].set(jnp.asarray(lengths, jnp.int32))

    lengths = jnp.where(number % 4 == 0, named(heavy_load, number // 4), named(common, number - number // 4 - 1))
    mixed = jax.random.permutation(jax.random.fold_in(own, 3), number_of)
    donor, receiver = mixed[0:number_of // 2 * 2:2], mixed[1:number_of // 2 * 2:2]
    margin = jnp.minimum(lengths[donor] - 1, reach - lengths[receiver]) // 2
    margin = jnp.where((donor == order[0]) | (receiver == order[0]) | (lengths[receiver] == 0), 0, jnp.maximum(margin, 0))
    shifted = jax.random.randint(jax.random.fold_in(own, 4), (number_of // 2,), 0, 1 << 20) % (margin + 1)
    lengths = lengths.at[donor].add(-shifted).at[receiver].add(shifted)
    labels = jnp.searchsorted(jnp.cumsum(lengths), jnp.arange(rows * top), side="right").astype(jnp.int32)
    listing = labels.reshape(top, rows).T
    listing = listing[jax.random.permutation(jax.random.fold_in(own, 1), rows)]
    rotation = jax.random.randint(jax.random.fold_in(own, 2), (rows, 1), 0, top)
    return jnp.take_along_axis(listing, (jnp.arange(top)[None, :] + rotation) % top, axis=1)


def portions_of(number_of, total, bound, skew, full):
    weights = [(1 << 20) // math.isqrt(rank ** skew) + 1 for rank in range(1, number_of + 1)]
    largest = bound if full else min(bound, max(-(-total // number_of), total * weights[0] // sum(weights)))
    least = 1 if total - largest >= number_of - 1 else 0
    counts, surplus = [largest] + [least] * (number_of - 1), total - largest - least * (number_of - 1)
    while surplus > 0:
        candidates = [i for i in range(1, number_of) if counts[i] < largest] or [i for i in range(1, number_of) if counts[i] < bound]
        whole, left = sum([weights[i] for i in candidates]), surplus
        for i in candidates:
            more = min(bound - counts[i], max(1, left * weights[i] // whole), surplus)
            counts[i] = counts[i] + more
            surplus = surplus - more
    return np.array(counts)


def bell_draw(key, dims, deviation, limit, split=(), kind=jnp.bfloat16):
    array = jax.random.normal(key, dims, jnp.float32) * deviation
    if len(split) > 0:
        array = block_levels(key, dims, split, -0.22, 0.18) * array
    return jnp.clip(array, min=-limit, max=limit).astype(kind)


def setup_inputs(seed: int = 0) -> dict:
    keys = jax.random.split(jax.random.key(seed), 15)
    tokens = bell_draw(keys[0], (BATCH, SEQ_LEN, D), 1.0, 6.0, ((0, 4), (1, 8)))
    cotangent = bell_draw(keys[1], (BATCH, SEQ_LEN, D), 1.0, 6.0, ((0, 4), (1, 8)))
    gain_attn = jnp.clip(1.0 + 0.1 * jax.random.normal(keys[2], (D,), jnp.float32), 0.5, 1.5).astype(jnp.bfloat16)
    query_w = bell_draw(keys[3], (D, INNER), (16 * D) ** -0.5, 0.0546875, ((0, 32),))
    key_w = bell_draw(keys[4], (D, INNER), D ** -0.5, 0.21875, ((0, 32),))
    value_w = bell_draw(keys[5], (D, INNER), D ** -0.5, 0.21875, ((0, 32),))
    output_w = bell_draw(keys[6], (INNER, D), (max(1, INNER // 32)) ** -0.5, 1.25, ((1, 32),))
    rel_table = bell_draw(keys[7], (BUCKETS, HEADS), 1.0, 4.0, ((0, 8),))
    rel_bucket = draw_rel_bucket(jax.random.fold_in(keys[14], 71), 0)
    gain_ffn = jnp.clip(1.0 + 0.1 * jax.random.normal(keys[9], (D,), jnp.float32), 0.5, 1.5).astype(jnp.bfloat16)
    router_w = bell_draw(keys[10], (D, EXPERTS), (2 * D) ** -0.5, 0.15625, ((0, 32),))
    routes_keys = jax.random.split(jax.random.fold_in(keys[11], 1), N_DP * N_SEQ * TOK_DEV // TOK_DEV)
    routes_turns = jax.random.permutation(jax.random.fold_in(keys[11], 3), N_DP * N_SEQ * TOK_DEV // TOK_DEV)
    routes = jax.vmap(lambda own, number: deal_out(jax.random.fold_in(keys[11], 2), own, number, TOK_DEV, EXPERTS, 1, CAP, 2))(routes_keys, routes_turns).reshape((N_DP, N_SEQ, TOK_DEV, 1))
    expert_in = bell_draw(keys[12], (EXPERTS, D, FF), D ** -0.5, 0.21875, ((0, 4), (2, 8)))
    expert_out = bell_draw(keys[13], (EXPERTS, D, FF), (max(1, FF // 256)) ** -0.5, 1.75, ((0, 4), (2, 8)))
    return dict(tokens=tokens, cotangent=cotangent, gain_attn=gain_attn, query_w=query_w, key_w=key_w, value_w=value_w, output_w=output_w, rel_table=rel_table, rel_bucket=rel_bucket, gain_ffn=gain_ffn, router_w=router_w, routes=routes, expert_in=expert_in, expert_out=expert_out)


epsilon = 1e-06
highest = lax.Precision.HIGHEST

@jax.custom_vjp
def low(v):
    return lax.optimization_barrier(v.astype(jnp.bfloat16)).astype(jnp.float32)

@jax.custom_vjp
def low_back(v):
    return v

def low_keep(v):
    return (low(v), None)

def low_pass(kept, grad):
    return (grad,)

def back_keep(v):
    return (v, None)

def back_low(kept, grad):
    return (low(grad),)
low.defvjp(low_keep, low_pass)
low_back.defvjp(back_keep, back_low)

def rms_norm(values, gain_vec):
    return values * lax.rsqrt(lax.optimization_barrier(jnp.mean(values * values, axis=-1, keepdims=True)) + epsilon) * gain_vec

def to_devices(array_in):
    trailing = array_in.shape[2:]
    split_view = array_in.reshape((N_DP, SEQS, N_SEQ, LOCAL) + trailing)
    perm_order = (0, 2, 1, 3) + tuple(range(4, 4 + len(trailing)))
    return split_view.transpose(perm_order).reshape((N_DP, N_SEQ, TOK_DEV) + trailing)

def to_sequences(array_in):
    trailing = array_in.shape[3:]
    split_view = array_in.reshape((N_DP, N_SEQ, SEQS, LOCAL) + trailing)
    perm_order = (0, 2, 1, 3) + tuple(range(4, 4 + len(trailing)))
    return split_view.transpose(perm_order).reshape((BATCH, SEQ_LEN) + trailing)

def reference(tokens, cotangent, gain_attn, query_w, key_w, value_w, output_w, rel_table, rel_bucket, gain_ffn, router_w, routes, expert_in, expert_out):
    route_dev = routes[..., 0].astype(jnp.int32)
    chosen = (route_dev[..., None] == jnp.arange(EXPERTS).astype(jnp.int32)).astype(jnp.int32)
    ranking = jnp.cumsum(chosen, axis=2) - chosen
    placed = (route_dev * CAP + lax.optimization_barrier(jnp.sum(ranking * chosen, axis=-1))).astype(jnp.int32)
    chosen_seq = to_sequences(chosen.astype(jnp.float32))
    dp_index = jnp.arange(N_DP).astype(jnp.int32)[:, None, None]
    seq_index = jnp.arange(N_SEQ).astype(jnp.int32)[None, :, None]
    offsets = (jnp.arange(SEQ_LEN)[None, :] - jnp.arange(SEQ_LEN)[:, None] + SEQ_LEN - 1).astype(jnp.int32)

    def forward(inputs, gain_a, w_query, w_key, w_value, w_out, bias_table, gain_f, w_router, w_up, w_down):
        normed_a = low(rms_norm(inputs, gain_a))

        def project(weight):
            return low(low_back(jnp.einsum('bld,de->ble', normed_a, weight, precision=highest)))
        queries = project(w_query)
        keys_all = project(w_key)
        values_all = project(w_value)
        bias_vec = bias_table[rel_bucket]
        bias_all = jnp.transpose(bias_vec[offsets], (2, 0, 1))

        def attend(triple):
            query_seq, key_seq, value_seq = triple
            query_h = query_seq.reshape(SEQ_LEN, HEADS, HEAD_DIM)
            key_h = key_seq.reshape(SEQ_LEN, HEADS, HEAD_DIM)
            value_h = value_seq.reshape(SEQ_LEN, HEADS, HEAD_DIM)
            scores = low_back(jnp.einsum('ihd,jhd->hij', query_h, key_h, precision=highest) + bias_all)
            weights = jax.nn.softmax(scores, axis=-1)
            context = jnp.einsum('hij,jhd->ihd', low(weights), value_h, precision=highest)
            return context.reshape(SEQ_LEN, INNER)
        context = low(low_back(lax.map(jax.checkpoint(attend), (queries, keys_all, values_all))))
        hidden_attn = inputs + low_back(jnp.einsum('ble,ed->bld', context, w_out, precision=highest))
        normed_f = low(rms_norm(hidden_attn, gain_f))
        logits = jnp.einsum('bld,de->ble', normed_f, w_router, precision=highest)
        gate_prob = lax.optimization_barrier(jnp.sum(jax.nn.softmax(logits, axis=-1) * chosen_seq, axis=-1))
        rows_dev = to_devices(normed_f)
        buffer = jnp.zeros((N_DP, N_SEQ, EXPERTS * CAP, D), jnp.float32).at[dp_index, seq_index, placed].set(rows_dev)
        by_expert = buffer.reshape(N_DP, N_SEQ, EXPERTS, CAP, D).transpose(2, 0, 1, 3, 4).reshape(EXPERTS, N_DP * N_SEQ * CAP, D)

        def expert_apply(triple):
            rows_in, w_in_e, w_out_e = triple
            pre_act = low_back(jnp.dot(rows_in, w_in_e, precision=highest))
            hidden = low(jax.nn.gelu(pre_act, approximate=True))
            return low(low_back(jnp.dot(hidden, w_out_e.T, precision=highest)))
        produced = lax.map(jax.checkpoint(expert_apply), (low_back(by_expert), w_up, w_down))
        returned = produced.reshape(EXPERTS, N_DP, N_SEQ, CAP, D).transpose(1, 2, 0, 3, 4).reshape(N_DP, N_SEQ, EXPERTS * CAP, D)
        expert_tok = to_sequences(returned[dp_index, seq_index, placed])
        return hidden_attn + gate_prob[..., None] * expert_tok
    primals = (tokens.astype(jnp.float32), gain_attn.astype(jnp.float32), query_w.astype(jnp.float32), key_w.astype(jnp.float32), value_w.astype(jnp.float32), output_w.astype(jnp.float32), rel_table.astype(jnp.float32), gain_ffn.astype(jnp.float32), router_w.astype(jnp.float32), expert_in.astype(jnp.float32), expert_out.astype(jnp.float32))
    mixed_out, pullback = jax.vjp(forward, *primals)
    gradients = pullback(cotangent.astype(jnp.float32))
    return (mixed_out.astype(jnp.bfloat16), gradients[0], gradients[1], gradients[2], gradients[3], gradients[4], gradients[5], gradients[6], gradients[7], gradients[8], gradients[9], gradients[10])
```

```python
import math
from functools import partial

import jax
import jax.numpy as jnp
from jax import lax
from jax.experimental import pallas as pl
from jax.experimental.pallas import tpu as pltpu
from jax.sharding import PartitionSpec as P

epsilon = 1e-06
highest = lax.Precision.HIGHEST
bf16 = jnp.bfloat16
f32 = jnp.float32
VMEM = 56 * 1024 * 1024


def dot_nn(left, right):
    return lax.dot_general(left, right, (((1,), (0,)), ((), ())), preferred_element_type=f32)


def dot_tn(left, right):
    return lax.dot_general(left, right, (((0,), (0,)), ((), ())), preferred_element_type=f32)


def dot_nt(left, right):
    return lax.dot_general(left, right, (((1,), (1,)), ((), ())), preferred_element_type=f32)


def swap(value, axis, mask):
    size = lax.axis_size(axis)
    return lax.ppermute(value, axis, [(i, i ^ mask) for i in range(size)])


def bits_of(size):
    return [1 << i for i in range(size.bit_length() - 1)]


def unxor(parts, index):
    for bit in bits_of(len(parts)):
        flag = (index & bit) != 0
        parts = [jnp.where(flag, parts[j ^ bit], parts[j]) for j in range(len(parts))]
    return parts


def grow(value, axis, mask, bit_set):
    other = swap(value, axis, mask)
    return jnp.stack([jnp.where(bit_set, other, value), jnp.where(bit_set, value, other)])


def pick(value, position, flag):
    low = lax.index_in_dim(value, 0, position, keepdims=False)
    high = lax.index_in_dim(value, 1, position, keepdims=False)
    return jnp.where(flag, high, low)


def halve(value, position, axis, mask, bit_set):
    sent = pick(value, position, jnp.logical_not(bit_set))
    kept = pick(value, position, bit_set)
    got = swap(sent, axis, mask)
    return (kept.astype(f32) + got.astype(f32)).astype(bf16)


def bias_tile(vec_ref, tile_ref, head):
    rows, width = tile_ref.shape
    vec = jnp.broadcast_to(vec_ref[pl.ds(head, 1), :], (rows, width))
    tile_ref[...] = pltpu.roll(vec, width - (rows - 1), 1, stride=1, stride_axis=0)


def key_columns(pos_ref, dims, query_z):
    n_z, n_y, local_len = dims
    z, y = pos_ref[0], pos_ref[1]
    query_block = (z ^ query_z) * n_y + y
    columns = []
    for key_y in range(n_y):
        for key_z in range(n_z):
            key_block = (z ^ key_z) * n_y + (y ^ key_y)
            first = (n_z * n_y - 1 - query_block + key_block) * local_len
            columns.append(pl.ds(pl.multiple_of(first, local_len), local_len))
    return columns


def split_keys(dims, seq_count, heads, size, kv_refs, offset, plain_ref, turned_ref):
    n_z, n_y, local_len = dims
    for head in range(heads):
        lo, hi = offset + head * size, offset + (head + 1) * size
        for s in range(seq_count):
            index = head * seq_count + s
            for key_y in range(n_y):
                for key_z in range(n_z):
                    at = (key_z * seq_count + s) * local_len
                    to = (key_y * n_z + key_z) * local_len
                    block = kv_refs[key_y][at : at + local_len, lo:hi]
                    if plain_ref is not None:
                        plain_ref[index, to : to + local_len, :] = block
                    if turned_ref is not None:
                        turned_ref[index, :, to : to + local_len] = block.T


def attn_fwd_kernel(dims, seq_count, heads, size, pos_ref, vec_ref, q_ref, *refs):
    n_z, n_y, local_len = dims
    kv_refs, (c_ref, lse_ref, tile_ref, kt_ref, v_ref, qh_ref, ch_ref) = refs[:n_y], refs[n_y:]
    inner = heads * size
    split_keys(dims, seq_count, heads, size, kv_refs, 0, None, kt_ref)
    split_keys(dims, seq_count, heads, size, kv_refs, inner, v_ref, None)
    for head in range(heads):
        qh_ref[head] = q_ref[:, head * size : (head + 1) * size]

    def head_step(head, carry):
        bias_tile(vec_ref, tile_ref, head)

        def query_step(query_z, carry):
            columns = key_columns(pos_ref, dims, query_z)
            for s in range(seq_count):
                row = pl.multiple_of((query_z * seq_count + s) * local_len, local_len)
                rows = pl.ds(row, local_len)
                bias = jnp.concatenate([tile_ref[:, c] for c in columns], axis=1)
                score = dot_nn(qh_ref[head, rows, :], kt_ref[head * seq_count + s]) + bias
                top = jnp.max(score, axis=1, keepdims=True)
                weight = jnp.exp(score - top)
                total = jnp.sum(weight, axis=1, keepdims=True)
                out = dot_nn(weight.astype(bf16), v_ref[head * seq_count + s])
                ch_ref[head, rows, :] = out / total
                lse_ref[head, rows, :] = top + jnp.log(total)
            return carry

        return lax.fori_loop(0, n_z, query_step, carry)

    lax.fori_loop(0, heads, head_step, 0)
    for head in range(heads):
        c_ref[:, head * size : (head + 1) * size] = ch_ref[head].astype(bf16)


def attn_bwd_kernel(dims, seq_count, heads, size, pos_ref, vec_ref, q_ref, dc_ref, lse_ref, *refs):
    n_z, n_y, local_len = dims
    kv_refs = refs[:n_y]
    dq_ref, diag_ref = refs[n_y], refs[n_y + 1]
    dkv_refs = refs[n_y + 2 : 2 * n_y + 2]
    refs = refs[2 * n_y + 2 :]
    tile_ref, grad_ref, kt_ref, vt_ref, k_ref, qh_ref, dch_ref, dqh_ref, dk_ref, dv_ref = refs
    inner = heads * size
    split_keys(dims, seq_count, heads, size, kv_refs, 0, k_ref, kt_ref)
    split_keys(dims, seq_count, heads, size, kv_refs, inner, None, vt_ref)
    for head in range(heads):
        qh_ref[head] = q_ref[:, head * size : (head + 1) * size]
        dch_ref[head] = dc_ref[:, head * size : (head + 1) * size]
    diag_ref[...] = jnp.zeros_like(diag_ref)
    dk_ref[...] = jnp.zeros_like(dk_ref)
    dv_ref[...] = jnp.zeros_like(dv_ref)

    def head_step(head, carry):
        bias_tile(vec_ref, tile_ref, head)
        grad_ref[...] = jnp.zeros_like(grad_ref)

        def query_step(query_z, carry):
            columns = key_columns(pos_ref, dims, query_z)
            for s in range(seq_count):
                index = head * seq_count + s
                row = pl.multiple_of((query_z * seq_count + s) * local_len, local_len)
                rows = pl.ds(row, local_len)
                q = qh_ref[head, rows, :]
                dc = dch_ref[head, rows, :]
                bias = jnp.concatenate([tile_ref[:, c] for c in columns], axis=1)
                prob = jnp.exp(dot_nn(q, kt_ref[index]) + bias - lse_ref[head, rows, :])
                dprob = dot_nn(dc, vt_ref[index])
                delta = jnp.sum(prob * dprob, axis=1, keepdims=True)
                ds = (prob * (dprob - delta)).astype(bf16)
                dqh_ref[head, rows, :] = dot_nn(ds, k_ref[index])
                dk_ref[index] += dot_tn(q, ds)
                dv_ref[index] += dot_tn(dc, prob.astype(bf16))
                for i, c in enumerate(columns):
                    part = ds[:, i * local_len : (i + 1) * local_len]
                    grad_ref[:, c] += part.astype(f32)
            return carry

        lax.fori_loop(0, n_z, query_step, 0)
        folded = grad_ref[...]
        width = folded.shape[1]
        while folded.shape[0] > 1:
            half = folded.shape[0] // 2
            folded = folded[:half] + pltpu.roll(folded[half:], width - half, 1)
        diag_ref[pl.ds(head, 1), :] = folded
        return carry

    lax.fori_loop(0, heads, head_step, 0)
    for head in range(heads):
        lo, hi = head * size, (head + 1) * size
        dq_ref[:, lo:hi] = dqh_ref[head].astype(bf16)
        for s in range(seq_count):
            index = head * seq_count + s
            for key_y in range(n_y):
                for key_z in range(n_z):
                    at = (key_z * seq_count + s) * local_len
                    to = (key_y * n_z + key_z) * local_len
                    out = dkv_refs[key_y]
                    cut = slice(to, to + local_len)
                    out[at : at + local_len, lo:hi] = dk_ref[index, :, cut].T.astype(out.dtype)
                    out[at : at + local_len, inner + lo : inner + hi] = dv_ref[
                        index, :, cut
                    ].T.astype(out.dtype)


def vmem_specs(count):
    return [pl.BlockSpec(memory_space=pltpu.VMEM) for _ in range(count)]


def attn_fwd(dims, seq_count, heads, size, pos, vec, q, kvs):
    rows = q.shape[0]
    length = dims[0] * dims[1] * dims[2]
    both = heads * seq_count
    return pl.pallas_call(
        partial(attn_fwd_kernel, dims, seq_count, heads, size),
        out_shape=(
            jax.ShapeDtypeStruct((rows, heads * size), bf16),
            jax.ShapeDtypeStruct((heads, rows, 1), f32),
        ),
        in_specs=[pl.BlockSpec(memory_space=pltpu.SMEM)] + vmem_specs(2 + len(kvs)),
        out_specs=tuple(vmem_specs(2)),
        scratch_shapes=[
            pltpu.VMEM((dims[2], vec.shape[1]), f32),
            pltpu.VMEM((both, size, length), bf16),
            pltpu.VMEM((both, length, size), bf16),
            pltpu.VMEM((heads, rows, size), bf16),
            pltpu.VMEM((heads, rows, size), f32),
        ],
        compiler_params=pltpu.CompilerParams(vmem_limit_bytes=VMEM),
        name="attn_fwd",
    )(pos, vec, q, *kvs)


def attn_bwd(dims, seq_count, heads, size, pos, vec, q, dc, lse, kvs):
    rows = q.shape[0]
    length = dims[0] * dims[1] * dims[2]
    both = heads * seq_count
    shapes = [jax.ShapeDtypeStruct((rows, heads * size), bf16), jax.ShapeDtypeStruct(vec.shape, f32)]
    for key_y in range(len(kvs)):
        shapes.append(jax.ShapeDtypeStruct(kvs[0].shape, f32 if key_y == 0 else bf16))
    return pl.pallas_call(
        partial(attn_bwd_kernel, dims, seq_count, heads, size),
        out_shape=tuple(shapes),
        in_specs=[pl.BlockSpec(memory_space=pltpu.SMEM)] + vmem_specs(4 + len(kvs)),
        out_specs=tuple(vmem_specs(len(shapes))),
        scratch_shapes=[
            pltpu.VMEM((dims[2], vec.shape[1]), f32),
            pltpu.VMEM((dims[2], vec.shape[1]), f32),
            pltpu.VMEM((both, size, length), bf16),
            pltpu.VMEM((both, size, length), bf16),
            pltpu.VMEM((both, length, size), bf16),
            pltpu.VMEM((heads, rows, size), bf16),
            pltpu.VMEM((heads, rows, size), bf16),
            pltpu.VMEM((heads, rows, size), f32),
            pltpu.VMEM((both, size, length), f32),
            pltpu.VMEM((both, size, length), f32),
        ],
        compiler_params=pltpu.CompilerParams(vmem_limit_bytes=VMEM),
        name="attn_bwd",
    )(pos, vec, q, dc, lse, *kvs)


def expert_kernel(rows_ref, dy_ref, up_ref, down_ref, y_ref, db_ref, g_ref, du_ref, y_acc, db_acc):
    step = pl.program_id(0)
    up = up_ref[0]
    down = down_ref[0]
    pre = dot_nn(rows_ref[...], up)
    square = pre * pre
    tanh = jnp.tanh(0.7978845608028654 * (pre + 0.044715 * pre * square))
    hidden = (0.5 * pre * (1.0 + tanh)).astype(bf16)
    slope = 0.5 * (1.0 + tanh) + 0.5 * pre * (1.0 - tanh * tanh) * (
        0.7978845608028654 * (1.0 + 0.134145 * square)
    )
    g_ref[0] = hidden
    y = dot_nt(hidden, down)
    du = (dot_nn(dy_ref[...], down) * slope).astype(bf16)
    du_ref[0] = du
    db = dot_nt(du, up)

    @pl.when(step == 0)
    def _():
        y_acc[...] = y
        db_acc[...] = db

    @pl.when(step > 0)
    def _():
        y_acc[...] += y
        db_acc[...] += db

    @pl.when(step == pl.num_programs(0) - 1)
    def _():
        y_ref[...] = y_acc[...].astype(bf16)
        db_ref[...] = db_acc[...].astype(bf16)


def expert_call(rows, dy, up, down):
    count, width = rows.shape
    n_z, _, hidden = up.shape
    whole = pl.BlockSpec((count, width), lambda i: (0, 0))
    weight = pl.BlockSpec((1, width, hidden), lambda i: (i, 0, 0))
    kept = pl.BlockSpec((1, count, hidden), lambda i: (i, 0, 0))
    return pl.pallas_call(
        expert_kernel,
        grid=(n_z,),
        out_shape=(
            jax.ShapeDtypeStruct((count, width), bf16),
            jax.ShapeDtypeStruct((count, width), bf16),
            jax.ShapeDtypeStruct((n_z, count, hidden), bf16),
            jax.ShapeDtypeStruct((n_z, count, hidden), bf16),
        ),
        in_specs=[whole, whole, weight, weight],
        out_specs=(whole, whole, kept, kept),
        scratch_shapes=[pltpu.VMEM((count, width), f32), pltpu.VMEM((count, width), f32)],
        compiler_params=pltpu.CompilerParams(vmem_limit_bytes=VMEM),
        name="expert",
    )(rows, dy, up, down)


def expert_grad_kernel(left_ref, right_ref, out_ref):
    out_ref[0] = dot_tn(left_ref[...], right_ref[0]).astype(bf16)


def expert_grad(left, right):
    count, width = left.shape
    n_z, _, hidden = right.shape
    return pl.pallas_call(
        expert_grad_kernel,
        grid=(n_z,),
        out_shape=jax.ShapeDtypeStruct((n_z, width, hidden), bf16),
        in_specs=[
            pl.BlockSpec((count, width), lambda i: (0, 0)),
            pl.BlockSpec((1, count, hidden), lambda i: (i, 0, 0)),
        ],
        out_specs=pl.BlockSpec((1, width, hidden), lambda i: (i, 0, 0)),
        compiler_params=pltpu.CompilerParams(vmem_limit_bytes=VMEM),
        name="expert_grad",
    )(left, right)


def local(
    tokens,
    cotangent,
    gain_attn,
    query_w,
    key_w,
    value_w,
    output_w,
    rel_table,
    rel_bucket,
    gain_ffn,
    router_w,
    routes,
    expert_in,
    expert_out,
):
    seq_count, local_len, width = tokens.shape
    tok = seq_count * local_len
    n_dp, n_seq = lax.axis_size("dp"), lax.axis_size("seq")
    head_count = rel_table.shape[1]
    inner = query_w.shape[1]
    size = inner // head_count
    n_z = math.gcd(head_count, n_seq)
    n_y = n_seq // n_z
    heads = head_count // n_z
    part = heads * size
    experts = router_w.shape[1]
    capacity = 2 * tok // experts
    table_rows = rel_table.shape[0]
    buckets = table_rows * n_seq
    w_rows = query_w.shape[0]
    dims = (n_z, n_y, local_len)
    dp, seq = lax.axis_index("dp"), lax.axis_index("seq")
    z, y = seq // n_y, seq % n_y
    dp_bits, y_bits, z_bits = bits_of(n_dp), bits_of(n_y), bits_of(n_z)

    def swap_z(value, k):
        return swap(value, "seq", k * n_y) if k else value

    def swap_y(value, k):
        return swap(value, "seq", k) if k else value

    def swap_dp(value, k):
        return swap(value, "dp", k) if k else value

    extra = jnp.concatenate([gain_attn[:, None], gain_ffn[:, None], router_w], axis=1)
    extra = jnp.broadcast_to(extra[None], (n_z, w_rows, 2 + experts))
    table_at = part * 3 + 2 + experts
    table = rel_table.reshape(table_rows, n_z, heads).transpose(1, 0, 2)
    table = jnp.pad(table, ((0, 0), (0, w_rows - table_rows), (0, 0)))
    joined = [w.reshape(w_rows, n_z, part).transpose(1, 0, 2) for w in (query_w, key_w, value_w)]
    pack = jnp.concatenate(joined + [extra, table], axis=2)
    packed = -(-pack.shape[2] // 128) * 128
    pack = jnp.pad(pack, ((0, 0), (0, 0), (0, packed - pack.shape[2])))
    by_partner = unxor([pack[j] for j in range(n_z)], z)
    gathered = jnp.stack(unxor([swap_z(by_partner[k], k) for k in range(n_z)], z))

    x_own = tokens.reshape(tok, width)
    x_parts = [swap_z(x_own, k) for k in range(n_z)]

    for bit in y_bits:
        gathered = grow(gathered, "seq", bit, (y & bit) != 0)
    for bit in reversed(dp_bits):
        gathered = grow(gathered, "dp", bit, (dp & bit) != 0)
    n_bits, m_bits = len(y_bits), len(dp_bits)
    order = tuple(reversed(range(m_bits))) + (m_bits + n_bits,)
    order = order + tuple(range(m_bits, m_bits + n_bits)) + (m_bits + n_bits + 1, m_bits + n_bits + 2)
    gathered = gathered.transpose(order).reshape(width, packed)
    w_qkv = gathered[:, : 3 * part]
    gain_a = gathered[:, 3 * part].astype(f32)
    gain_f = gathered[:, 3 * part + 1].astype(f32)
    w_router = gathered[:, 3 * part + 2 : 3 * part + 2 + experts]
    table = gathered.reshape(n_dp, n_seq, w_rows, packed)[0, :, :table_rows, table_at : table_at + heads]
    table = table.reshape(buckets, heads)

    out_t = output_w.T
    for bit in z_bits:
        out_t = grow(out_t, "seq", bit * n_y, (z & bit) != 0)
    for bit in y_bits:
        out_t = grow(out_t, "seq", bit, (y & bit) != 0)
    for bit in reversed(dp_bits):
        out_t = grow(out_t, "dp", bit, (dp & bit) != 0)
    l_bits = len(z_bits)
    order = tuple(reversed(range(m_bits)))
    order = order + tuple(range(m_bits + n_bits, m_bits + n_bits + l_bits))
    order = order + tuple(range(m_bits, m_bits + n_bits))
    order = order + (m_bits + n_bits + l_bits, m_bits + n_bits + l_bits + 1)
    out_t = out_t.transpose(order).reshape(width, inner)

    z_groups = [[j * n_y + i for j in range(n_z)] for i in range(n_y)]
    up = lax.all_gather(expert_in[0], "seq", axis=0, axis_index_groups=z_groups)
    down = lax.all_gather(expert_out[0], "seq", axis=0, axis_index_groups=z_groups)

    route_ids = routes.reshape(tok)
    choose = route_ids[:, None] == jnp.arange(experts, dtype=jnp.int32)[None, :]
    choose_f = choose.astype(f32)
    before = jnp.arange(tok)[:, None] > jnp.arange(tok)[None, :]
    earlier = dot_nn(before.astype(bf16), choose.astype(bf16))
    slot = jnp.sum(earlier * choose_f, axis=1).astype(jnp.int32)
    place = (route_ids ^ dp) * capacity + slot
    place_hot = jnp.arange(experts * capacity, dtype=jnp.int32)[:, None] == place[None, :]
    place_b = place_hot.astype(bf16)

    def to_experts(values):
        sent = dot_nn(place_b, values).astype(bf16).reshape(experts, capacity, width)
        got = [swap_dp(sent[k], k) for k in range(n_dp)]
        return [[swap_y(v, k) for v in got] for k in range(n_y)]

    def from_experts(values):
        split = values.reshape(n_y, n_dp * capacity, width)
        total = split[0].astype(f32)
        for k in range(1, n_y):
            total = total + swap_y(split[k], k).astype(f32)
        blocks = total.astype(bf16).reshape(n_dp, capacity, width)
        back = [swap_dp(blocks[k], k) for k in range(n_dp)]
        return dot_tn(place_b, jnp.concatenate(back, axis=0))

    upstream_b = cotangent.reshape(tok, width)
    upstream = upstream_b.astype(f32)
    d_rows = to_experts(upstream_b)

    x_all = jnp.concatenate(x_parts, axis=0).astype(f32)
    scale_all = lax.rsqrt(jnp.mean(x_all * x_all, axis=-1, keepdims=True) + epsilon)
    normed_all = (x_all * scale_all * gain_a).astype(bf16)
    kv = dot_nn(normed_all, w_qkv[:, part:]).astype(bf16)
    kvs = [swap_y(kv, k) for k in range(n_y)]
    q = dot_nn(normed_all, w_qkv[:, :part]).astype(bf16)
    span = 2 * n_seq * local_len
    bucket_pad = jnp.concatenate([rel_bucket, jnp.full((1,), -1, jnp.int32)])
    bucket_hot = bucket_pad[None, :] == jnp.arange(buckets, dtype=jnp.int32)[:, None]
    table_pad = jnp.pad(table, ((0, 0), (0, 8 - heads)))
    vec = dot_tn(table_pad, bucket_hot.astype(bf16))
    pos = jnp.stack([z, y]).astype(jnp.int32)
    context_parts, lse = attn_fwd(dims, seq_count, heads, size, pos, vec, q, kvs)
    context_parts = context_parts.reshape(n_z, tok, part)
    context = [swap_z(context_parts[k], k) for k in range(n_z)]
    context = jnp.concatenate(unxor(context, z), axis=1)

    inputs = x_own.astype(f32)
    hidden_attn = inputs + dot_nt(context, out_t)
    scale_f = lax.rsqrt(jnp.mean(hidden_attn * hidden_attn, axis=-1, keepdims=True) + epsilon)
    normed_f = (hidden_attn * scale_f * gain_f).astype(bf16)
    logits = dot_nn(normed_f, w_router)
    router_p = jax.nn.softmax(logits, axis=-1)
    gate = jnp.sum(router_p * choose_f, axis=-1)

    b_rows = to_experts(normed_f)
    gate_rows = jnp.sum(jnp.where(place_hot, gate[None, :], 0.0), axis=1).reshape(experts, capacity)
    gate_rows = jnp.concatenate([swap_dp(gate_rows[k], k) for k in range(n_dp)])
    gate_rows = jnp.concatenate([swap_y(gate_rows, k) for k in range(n_y)])
    rows = jnp.concatenate([v for group in b_rows for v in group], axis=0)
    dy = jnp.concatenate([v for group in d_rows for v in group], axis=0)
    dy = (dy.astype(f32) * gate_rows[:, None]).astype(bf16)
    y_part, db_part, hidden, grad_pre = expert_call(rows, dy, up, down)
    grad_normed = from_experts(db_part)
    expert_tok = from_experts(y_part)
    grad_up = expert_grad(rows, grad_pre)
    grad_down = expert_grad(dy, hidden)
    grad_up = lax.psum_scatter(
        grad_up, "seq", scatter_dimension=0, axis_index_groups=z_groups, tiled=True
    ).astype(f32)
    grad_down = lax.psum_scatter(
        grad_down, "seq", scatter_dimension=0, axis_index_groups=z_groups, tiled=True
    ).astype(f32)

    mixed = (hidden_attn + gate[:, None] * expert_tok).astype(bf16).reshape(tokens.shape)
    grad_gate = jnp.sum(upstream * expert_tok, axis=-1)
    grad_logits = grad_gate[:, None] * router_p * (choose_f - gate[:, None])
    grad_router = lax.dot_general(
        normed_f.astype(f32), grad_logits, (((0,), (0,)), ((), ())), precision=highest
    )
    grad_normed = grad_normed + lax.dot_general(
        grad_logits, w_router.astype(f32), (((1,), (1,)), ((), ())), precision=highest
    )
    scaled = gain_f * grad_normed
    grad_hidden = upstream + scale_f * scaled
    grad_hidden = grad_hidden - hidden_attn * scale_f**3 * jnp.mean(
        scaled * hidden_attn, axis=-1, keepdims=True
    )
    grad_gain_f = jnp.sum(grad_normed * hidden_attn * scale_f, axis=0)
    grad_attn = grad_hidden.astype(bf16)

    grad_ctx = dot_nn(grad_attn, out_t).astype(bf16)
    grad_ctx = unxor([grad_ctx[:, j * part : (j + 1) * part] for j in range(n_z)], z)
    grad_ctx = jnp.concatenate([swap_z(grad_ctx[k], k) for k in range(n_z)], axis=0)
    grad_q, diag, *grad_kvs = attn_bwd(
        dims, seq_count, heads, size, pos, vec, q, grad_ctx, lse, kvs
    )
    grad_kv = grad_kvs[0]
    for k in range(1, n_y):
        grad_kv = grad_kv + swap_y(grad_kvs[k], k).astype(f32)
    grad_qkv = jnp.concatenate([grad_q, grad_kv.astype(bf16)], axis=1)
    grad_a_part = dot_nt(grad_qkv, w_qkv)
    grad_a_parts = grad_a_part.reshape(n_z, tok, width)
    grad_a = grad_a_parts[0]
    for k in range(1, n_z):
        grad_a = grad_a + swap_z(grad_a_parts[k].astype(bf16), k).astype(f32)
    scale_a = scale_all[:tok]
    scaled_a = gain_a * grad_a
    grad_x = grad_hidden + scale_a * scaled_a
    grad_x = grad_x - inputs * scale_a**3 * jnp.mean(scaled_a * inputs, axis=-1, keepdims=True)
    grad_tokens = grad_x.reshape(tokens.shape)

    def scatter(value, z_halves):
        columns = value.shape[1]
        shape = (2,) * m_bits + ((2,) * l_bits if z_halves else (n_z,)) + (2,) * n_bits
        value = value.astype(bf16).reshape(shape + (w_rows, columns))
        axes = list(range(m_bits))
        for bit in dp_bits:
            value = halve(value, len(axes) - 1, "dp", bit, (dp & bit) != 0)
            axes.pop()
        z_axes = l_bits if z_halves else 1
        for i, bit in enumerate(y_bits):
            value = halve(value, z_axes + n_bits - 1 - i, "seq", bit, (y & bit) != 0)
        if z_halves:
            for i, bit in enumerate(z_bits):
                value = halve(value, l_bits - 1 - i, "seq", bit * n_y, (z & bit) != 0)
            return value
        parts = unxor([value[j] for j in range(n_z)], z)
        return unxor([swap_z(parts[k], k) for k in range(n_z)], z)

    grad_out_t = dot_tn(grad_attn, context)
    grad_f = jnp.concatenate([grad_gain_f[:, None], grad_router], axis=1)
    grad_f = jnp.pad(grad_f, ((0, 0), (0, 128 - grad_f.shape[1])))
    summed_f = scatter(jnp.concatenate([grad_out_t, grad_f], axis=1), True).astype(f32)
    grad_output = summed_f[:, :inner].T
    grad_gain_ffn = summed_f[:, inner]
    grad_router = summed_f[:, inner + 1 : inner + 1 + experts]

    grad_w = dot_tn(normed_all, grad_qkv)
    grad_gain_a = jnp.sum(grad_a_part * x_all * scale_all, axis=0)
    diag = jnp.roll(diag, local_len - 1, axis=1)
    grad_table = lax.dot_general(
        diag, bucket_hot.astype(f32), (((1,), (1,)), ((), ())), precision=highest
    )
    grad_table = grad_table[:heads].T.reshape(1, n_seq, table_rows, heads)
    grad_table = jnp.pad(grad_table, ((0, 0), (0, 0), (0, w_rows - table_rows), (0, 0)))
    grad_table = jnp.broadcast_to(grad_table, (n_dp, n_seq, w_rows, heads)).reshape(width, heads)
    grad_e = jnp.concatenate([grad_gain_a[:, None], grad_table], axis=1)
    grad_e = jnp.pad(grad_e, ((0, 0), (0, packed - 3 * part - grad_e.shape[1])))
    summed = scatter(jnp.concatenate([grad_w, grad_e], axis=1), False)
    grad_query, grad_key, grad_value = (
        jnp.concatenate([v[:, i * part : (i + 1) * part] for v in summed], axis=1).astype(f32)
        for i in range(3)
    )
    grad_gain_attn = sum(v[:, 3 * part].astype(f32) for v in summed)
    grad_table = jnp.concatenate(
        [v[:table_rows, 3 * part + 1 : 3 * part + 1 + heads] for v in summed], axis=1
    ).astype(f32)

    return (
        mixed,
        grad_tokens,
        grad_gain_attn,
        grad_query,
        grad_key,
        grad_value,
        grad_output,
        grad_table,
        grad_gain_ffn,
        grad_router,
        grad_up,
        grad_down,
    )


def solution(mesh):
    vector = P(("dp", "seq"))
    matrix = P(("dp", "seq"), None)
    rows = P("dp", "seq", None)
    expert = P("dp", None, "seq")
    last = P(None, ("dp", "seq"))
    table = P("seq", None)
    return jax.shard_map(
        local,
        mesh=mesh,
        in_specs=(
            rows,
            rows,
            vector,
            matrix,
            matrix,
            matrix,
            last,
            table,
            P(),
            vector,
            matrix,
            P("dp", "seq", None, None),
            expert,
            expert,
        ),
        out_specs=(
            rows,
            rows,
            vector,
            matrix,
            matrix,
            matrix,
            last,
            table,
            vector,
            matrix,
            expert,
            expert,
        ),
        check_vma=False,
    )
```

```python
import math
from functools import partial

import jax
import jax.numpy as jnp
from jax import lax
from jax.experimental import pallas as pl
from jax.experimental.pallas import tpu as pltpu
from jax.sharding import PartitionSpec as P

epsilon = 1e-06
highest = lax.Precision.HIGHEST
bf16 = jnp.bfloat16
f32 = jnp.float32
VMEM = 56 * 1024 * 1024


def dot_nn(left, right):
    return lax.dot_general(left, right, (((1,), (0,)), ((), ())), preferred_element_type=f32)


def dot_tn(left, right):
    return lax.dot_general(left, right, (((0,), (0,)), ((), ())), preferred_element_type=f32)


def dot_nt(left, right):
    return lax.dot_general(left, right, (((1,), (1,)), ((), ())), preferred_element_type=f32)


def swap(value, axis, mask):
    size = lax.axis_size(axis)
    return lax.ppermute(value, axis, [(i, i ^ mask) for i in range(size)])


def bits_of(size):
    return [1 << i for i in range(size.bit_length() - 1)]


def unxor(parts, index):
    for bit in bits_of(len(parts)):
        flag = (index & bit) != 0
        parts = [jnp.where(flag, parts[j ^ bit], parts[j]) for j in range(len(parts))]
    return parts


def after(value, *others):
    return lax.optimization_barrier((value, *others))[0]


def grow(value, axis, mask, bit_set):
    other = swap(value, axis, mask)
    return jnp.stack([jnp.where(bit_set, other, value), jnp.where(bit_set, value, other)])


def pick(value, position, flag):
    low = lax.index_in_dim(value, 0, position, keepdims=False)
    high = lax.index_in_dim(value, 1, position, keepdims=False)
    return jnp.where(flag, high, low)


def halve(value, position, axis, mask, bit_set):
    sent = pick(value, position, jnp.logical_not(bit_set))
    kept = pick(value, position, bit_set)
    got = swap(sent, axis, mask)
    return (kept.astype(f32) + got.astype(f32)).astype(bf16)


def bias_tile(vec_ref, tile_ref, head):
    rows, width = tile_ref.shape
    vec = jnp.broadcast_to(vec_ref[pl.ds(head, 1), :], (rows, width))
    tile_ref[...] = pltpu.roll(vec, width - (rows - 1), 1, stride=1, stride_axis=0)


def key_columns(pos_ref, dims, key_ys, query_z):
    n_z, n_y, local_len = dims
    z, y = pos_ref[0], pos_ref[1]
    query_block = (z ^ query_z) * n_y + y
    columns = []
    for key_y in key_ys:
        for key_z in range(n_z):
            key_block = (z ^ key_z) * n_y + (y ^ key_y)
            first = (n_z * n_y - 1 - query_block + key_block) * local_len
            columns.append(pl.ds(pl.multiple_of(first, local_len), local_len))
    return columns


def split_keys(dims, seq_count, heads, size, kv_refs, offset, plain_ref, turned_ref):
    n_z, _, local_len = dims
    for head in range(heads):
        lo, hi = offset + head * size, offset + (head + 1) * size
        for s in range(seq_count):
            index = head * seq_count + s
            for group, kv_ref in enumerate(kv_refs):
                for key_z in range(n_z):
                    at = (key_z * seq_count + s) * local_len
                    to = (group * n_z + key_z) * local_len
                    block = kv_ref[at : at + local_len, lo:hi]
                    if plain_ref is not None:
                        plain_ref[index, to : to + local_len, :] = block
                    if turned_ref is not None:
                        turned_ref[index, :, to : to + local_len] = block.T


def attn_fwd_kernel(dims, seq_count, heads, size, key_ys, first, pos_ref, vec_ref, q_ref, *refs):
    n_z, _, local_len = dims
    kv_refs, refs = refs[: len(key_ys)], refs[len(key_ys) :]
    if first:
        out_ref, *refs = refs
    else:
        out_in, c_ref, out_ref, *refs = refs
    tile_ref, kt_ref, v_ref, qh_ref = refs
    inner = heads * size
    split_keys(dims, seq_count, heads, size, kv_refs, 0, None, kt_ref)
    split_keys(dims, seq_count, heads, size, kv_refs, inner, v_ref, None)
    for head in range(heads):
        qh_ref[head] = q_ref[:, head * size : (head + 1) * size]

    def head_step(head, carry):
        bias_tile(vec_ref, tile_ref, head)

        def query_step(query_z, carry):
            columns = key_columns(pos_ref, dims, key_ys, query_z)
            for s in range(seq_count):
                row = pl.multiple_of((query_z * seq_count + s) * local_len, local_len)
                rows = pl.ds(row, local_len)
                bias = jnp.concatenate([tile_ref[:, c] for c in columns], axis=1)
                score = dot_nn(qh_ref[head, rows, :], kt_ref[head * seq_count + s]) + bias
                top = jnp.max(score, axis=1, keepdims=True)
                if not first:
                    top_before = out_in[head, rows, size : size + 1]
                    top = jnp.maximum(top, top_before)
                weight = jnp.exp(score - top)
                total = jnp.sum(weight, axis=1, keepdims=True)
                out = dot_nn(weight.astype(bf16), v_ref[head * seq_count + s])
                if first:
                    out_ref[head, rows, :size] = out
                    out_ref[head, rows, size : size + 1] = top
                    out_ref[head, rows, size + 1 : size + 2] = total
                else:
                    fade = jnp.exp(top_before - top)
                    total = total + fade * out_in[head, rows, size + 1 : size + 2]
                    out_ref[head, rows, :size] = (out + fade * out_in[head, rows, :size]) / total
                    out_ref[head, rows, size : size + 1] = top + jnp.log(total)
            return carry

        return lax.fori_loop(0, n_z, query_step, carry)

    lax.fori_loop(0, heads, head_step, 0)
    if not first:
        for head in range(heads):
            c_ref[:, head * size : (head + 1) * size] = out_ref[head, :, :size].astype(bf16)


def attn_bwd_kernel(dims, seq_count, heads, size, key_ys, first, pos_ref, vec_ref, q_ref, *refs):
    n_z, _, local_len = dims
    count = len(key_ys)
    dc_ref, c_ref, *refs = refs
    kv_refs, refs = refs[:count], refs[count:]
    if first:
        dq_ref, diag_ref, *refs = refs
        dqh_ref = dq_ref
    else:
        dq_in, diag_in, dq_ref, diag_ref, *refs = refs
    dkv_refs, refs = refs[:count], refs[count:]
    tile_ref, grad_ref, kt_ref, vt_ref, k_ref, qh_ref, dch_ref, delta_ref, dk_ref, dv_ref = refs[:10]
    if not first:
        dqh_ref = refs[10]
    inner = heads * size
    split_keys(dims, seq_count, heads, size, kv_refs, 0, k_ref, kt_ref)
    split_keys(dims, seq_count, heads, size, kv_refs, inner, None, vt_ref)
    for head in range(heads):
        qh_ref[head] = q_ref[:, head * size : (head + 1) * size]
        dc = dc_ref[:, head * size : (head + 1) * size]
        dch_ref[head] = dc
        delta_ref[head] = jnp.sum(dc.astype(f32) * c_ref[head, :, :size], axis=1, keepdims=True)
    if first:
        diag_ref[...] = jnp.zeros_like(diag_ref)
    else:
        diag_ref[...] = diag_in[...]
    dk_ref[...] = jnp.zeros_like(dk_ref)
    dv_ref[...] = jnp.zeros_like(dv_ref)

    def head_step(head, carry):
        bias_tile(vec_ref, tile_ref, head)
        grad_ref[...] = jnp.zeros_like(grad_ref)

        def query_step(query_z, carry):
            columns = key_columns(pos_ref, dims, key_ys, query_z)
            for s in range(seq_count):
                index = head * seq_count + s
                row = pl.multiple_of((query_z * seq_count + s) * local_len, local_len)
                rows = pl.ds(row, local_len)
                q = qh_ref[head, rows, :]
                dc = dch_ref[head, rows, :]
                bias = jnp.concatenate([tile_ref[:, c] for c in columns], axis=1)
                prob = jnp.exp(dot_nn(q, kt_ref[index]) + bias - c_ref[head, rows, size : size + 1])
                dprob = dot_nn(dc, vt_ref[index])
                ds = (prob * (dprob - delta_ref[head, rows, :])).astype(bf16)
                dq = dot_nn(ds, k_ref[index])
                if not first:
                    dq = dq + dq_in[head, rows, :]
                dqh_ref[head, rows, :] = dq
                dk_ref[index] += dot_tn(q, ds)
                dv_ref[index] += dot_tn(dc, prob.astype(bf16))
                for i, c in enumerate(columns):
                    part = ds[:, i * local_len : (i + 1) * local_len]
                    grad_ref[:, c] += part.astype(f32)
            return carry

        lax.fori_loop(0, n_z, query_step, 0)
        folded = grad_ref[...]
        width = folded.shape[1]
        while folded.shape[0] > 1:
            half = folded.shape[0] // 2
            folded = folded[:half] + pltpu.roll(folded[half:], width - half, 1)
        diag_ref[pl.ds(head, 1), :] += folded
        return carry

    lax.fori_loop(0, heads, head_step, 0)
    for head in range(heads):
        lo, hi = head * size, (head + 1) * size
        if not first:
            dq_ref[:, lo:hi] = dqh_ref[head].astype(bf16)
        for s in range(seq_count):
            index = head * seq_count + s
            for group, out in enumerate(dkv_refs):
                for key_z in range(n_z):
                    at = (key_z * seq_count + s) * local_len
                    to = (group * n_z + key_z) * local_len
                    cut = slice(to, to + local_len)
                    out[at : at + local_len, lo:hi] = dk_ref[index, :, cut].T.astype(out.dtype)
                    out[at : at + local_len, inner + lo : inner + hi] = dv_ref[
                        index, :, cut
                    ].T.astype(out.dtype)


def vmem_specs(count):
    return [pl.BlockSpec(memory_space=pltpu.VMEM) for _ in range(count)]


def attn_fwd(dims, seq_count, heads, size, key_ys, pos, vec, q, kvs, before=()):
    rows = q.shape[0]
    length = len(key_ys) * dims[0] * dims[2]
    both = heads * seq_count
    first = not before
    wide = jax.ShapeDtypeStruct((heads, rows, 2 * size), f32)
    joined = jax.ShapeDtypeStruct((rows, heads * size), bf16)
    return pl.pallas_call(
        partial(attn_fwd_kernel, dims, seq_count, heads, size, key_ys, first),
        out_shape=(wide,) if first else (joined, wide),
        in_specs=[pl.BlockSpec(memory_space=pltpu.SMEM)]
        + vmem_specs(2 + len(kvs) + len(before)),
        out_specs=tuple(vmem_specs(1 if first else 2)),
        scratch_shapes=[
            pltpu.VMEM((dims[2], vec.shape[1]), f32),
            pltpu.VMEM((both, size, length), bf16),
            pltpu.VMEM((both, length, size), bf16),
            pltpu.VMEM((heads, rows, size), bf16),
        ],
        compiler_params=pltpu.CompilerParams(vmem_limit_bytes=VMEM),
        name="attn_fwd",
    )(pos, vec, q, *kvs, *before)


def attn_bwd(dims, seq_count, heads, size, key_ys, pos, vec, q, dc, c, kvs, before=()):
    rows = q.shape[0]
    length = len(key_ys) * dims[0] * dims[2]
    both = heads * seq_count
    first = not before
    wide = jax.ShapeDtypeStruct((heads, rows, size), f32)
    joined = jax.ShapeDtypeStruct((rows, heads * size), bf16)
    shapes = [wide if first else joined, jax.ShapeDtypeStruct(vec.shape, f32)]
    for key_y in key_ys:
        shapes.append(jax.ShapeDtypeStruct(kvs[0].shape, bf16 if key_y else f32))
    scratch = [
        pltpu.VMEM((dims[2], vec.shape[1]), f32),
        pltpu.VMEM((dims[2], vec.shape[1]), f32),
        pltpu.VMEM((both, size, length), bf16),
        pltpu.VMEM((both, size, length), bf16),
        pltpu.VMEM((both, length, size), bf16),
        pltpu.VMEM((heads, rows, size), bf16),
        pltpu.VMEM((heads, rows, size), bf16),
        pltpu.VMEM((heads, rows, 1), f32),
        pltpu.VMEM((both, size, length), f32),
        pltpu.VMEM((both, size, length), f32),
    ]
    if not first:
        scratch.append(pltpu.VMEM((heads, rows, size), f32))
    return pl.pallas_call(
        partial(attn_bwd_kernel, dims, seq_count, heads, size, key_ys, first),
        out_shape=tuple(shapes),
        in_specs=[pl.BlockSpec(memory_space=pltpu.SMEM)]
        + vmem_specs(4 + len(kvs) + len(before)),
        out_specs=tuple(vmem_specs(len(shapes))),
        scratch_shapes=scratch,
        compiler_params=pltpu.CompilerParams(vmem_limit_bytes=VMEM),
        name="attn_bwd",
    )(pos, vec, q, dc, c, *kvs, *before)


def gelu_parts(pre):
    square = pre * pre
    tanh = jnp.tanh(0.7978845608028654 * (pre + 0.044715 * pre * square))
    hidden = 0.5 * pre * (1.0 + tanh)
    slope = 0.5 * (1.0 + tanh) + 0.5 * pre * (1.0 - tanh * tanh) * (
        0.7978845608028654 * (1.0 + 0.134145 * square)
    )
    return hidden.astype(bf16), slope


def accumulate(out_ref, acc_ref, value):
    step = pl.program_id(0)

    @pl.when(step == 0)
    def _():
        acc_ref[...] = value

    @pl.when(step > 0)
    def _():
        acc_ref[...] += value

    @pl.when(step == pl.num_programs(0) - 1)
    def _():
        out_ref[...] = acc_ref[...].astype(out_ref.dtype)


def expert_own_kernel(rows_ref, dy_ref, weight_ref, y_ref, db_ref, g_ref, du_ref, y_acc, db_acc):
    hidden, slope = gelu_parts(dot_nn(rows_ref[...], weight_ref[0, 0]))
    g_ref[0] = hidden
    accumulate(y_ref, y_acc, dot_nt(hidden, weight_ref[0, 1]))
    du = (dot_nn(dy_ref[...], weight_ref[0, 1]) * slope).astype(bf16)
    du_ref[0] = du
    accumulate(db_ref, db_acc, dot_nt(du, weight_ref[0, 0]))


def expert_fwd_kernel(rows_ref, weight_ref, y_ref, g_ref, slope_ref, y_acc):
    hidden, slope = gelu_parts(dot_nn(rows_ref[...], weight_ref[0, 0]))
    g_ref[0] = hidden
    slope_ref[0] = slope.astype(bf16)
    accumulate(y_ref, y_acc, dot_nt(hidden, weight_ref[0, 1]))


def expert_bwd_kernel(dy_ref, slope_ref, weight_ref, db_ref, du_ref, db_acc):
    du = (dot_nn(dy_ref[...], weight_ref[0, 1]) * slope_ref[0].astype(f32)).astype(bf16)
    du_ref[0] = du
    accumulate(db_ref, db_acc, dot_nt(du, weight_ref[0, 0]))


def expert_call(kernel, name, rows, kept_in, up_down, out_type, wholes):
    count = rows[0].shape[0]
    n_z, _, width, hidden = up_down.shape
    whole = pl.BlockSpec((count, width), lambda i: (0, 0))
    weight = pl.BlockSpec((1, 2, width, hidden), lambda i: (i, 0, 0, 0))
    kept = pl.BlockSpec((1, count, hidden), lambda i: (i, 0, 0))
    kept_out = 1 if kept_in else 2
    return pl.pallas_call(
        kernel,
        grid=(n_z,),
        out_shape=(jax.ShapeDtypeStruct((count, width), out_type),) * wholes
        + (jax.ShapeDtypeStruct((n_z, count, hidden), bf16),) * kept_out,
        in_specs=[whole] * len(rows) + [kept] * len(kept_in) + [weight],
        out_specs=(whole,) * wholes + (kept,) * kept_out,
        scratch_shapes=[pltpu.VMEM((count, width), f32)] * wholes,
        compiler_params=pltpu.CompilerParams(vmem_limit_bytes=VMEM),
        name=name,
    )(*rows, *kept_in, up_down)


def expert_grad_kernel(b_ref, b_other, dy_ref, dy_other, du_ref, du_other, g_ref, g_other, out_ref):
    grad_up = dot_tn(b_ref[...], du_ref[0]) + dot_tn(b_other[...], du_other[0])
    out_ref[0, 0] = grad_up.astype(bf16)
    grad_down = dot_tn(dy_ref[...], g_ref[0]) + dot_tn(dy_other[...], g_other[0])
    out_ref[0, 1] = grad_down.astype(bf16)


def expert_grad(rows, kept):
    width = rows[2].shape[1]
    n_z, _, hidden = kept[0].shape
    return pl.pallas_call(
        expert_grad_kernel,
        grid=(n_z,),
        out_shape=jax.ShapeDtypeStruct((n_z, 2, width, hidden), bf16),
        in_specs=[pl.BlockSpec((v.shape[0], width), lambda i: (0, 0)) for v in rows]
        + [pl.BlockSpec((1,) + v.shape[1:], lambda i: (i, 0, 0)) for v in kept],
        out_specs=pl.BlockSpec((1, 2, width, hidden), lambda i: (i, 0, 0, 0)),
        compiler_params=pltpu.CompilerParams(vmem_limit_bytes=VMEM),
        name="expert_grad",
    )(*rows, *kept)


def weight_grad_kernel(a_ref, grad_ref, out_grad_ref, context_ref, small_ref, out_ref):
    cut = grad_ref.shape[1]
    wide = cut + small_ref.shape[1]
    out_ref[:, :cut] = dot_tn(a_ref[...], grad_ref[...]).astype(bf16)
    out_ref[:, cut:wide] = small_ref[...].astype(bf16)
    out_ref[:, wide:] = dot_tn(out_grad_ref[...], context_ref[...]).astype(bf16)


def weight_grad(a, grad, out_grad, context, small):
    width = a.shape[1]
    columns = grad.shape[1] + small.shape[1] + context.shape[1]
    return pl.pallas_call(
        weight_grad_kernel,
        out_shape=jax.ShapeDtypeStruct((width, columns), bf16),
        in_specs=vmem_specs(5),
        out_specs=vmem_specs(1)[0],
        compiler_params=pltpu.CompilerParams(vmem_limit_bytes=VMEM),
        name="weight_grad",
    )(a, grad, out_grad, context, small)


def local(
    tokens,
    cotangent,
    gain_attn,
    query_w,
    key_w,
    value_w,
    output_w,
    rel_table,
    rel_bucket,
    gain_ffn,
    router_w,
    routes,
    expert_in,
    expert_out,
):
    seq_count, local_len, width = tokens.shape
    tok = seq_count * local_len
    n_dp, n_seq = lax.axis_size("dp"), lax.axis_size("seq")
    head_count = rel_table.shape[1]
    inner = query_w.shape[1]
    size = inner // head_count
    n_z = math.gcd(head_count, n_seq)
    n_y = n_seq // n_z
    heads = head_count // n_z
    part = heads * size
    experts = router_w.shape[1]
    capacity = 2 * tok // experts
    table_rows = rel_table.shape[0]
    buckets = table_rows * n_seq
    w_rows = query_w.shape[0]
    dims = (n_z, n_y, local_len)
    dp, seq = lax.axis_index("dp"), lax.axis_index("seq")
    z, y = seq // n_y, seq % n_y
    dp_bits, y_bits, z_bits = bits_of(n_dp), bits_of(n_y), bits_of(n_z)

    def swap_z(value, k):
        return swap(value, "seq", k * n_y) if k else value

    def swap_y(value, k):
        return swap(value, "seq", k) if k else value

    def swap_dp(value, k):
        return swap(value, "dp", k) if k else value

    extra = jnp.concatenate([gain_attn[:, None], gain_ffn[:, None], router_w], axis=1)
    extra = jnp.broadcast_to(extra[None], (n_z, w_rows, 2 + experts))
    table_at = part * 3 + 2 + experts
    table = rel_table.reshape(table_rows, n_z, heads).transpose(1, 0, 2)
    table = jnp.pad(table, ((0, 0), (0, w_rows - table_rows), (0, 0)))
    joined = [w.reshape(w_rows, n_z, part).transpose(1, 0, 2) for w in (query_w, key_w, value_w)]
    pack = jnp.concatenate(joined + [extra, table], axis=2)
    packed = -(-pack.shape[2] // 128) * 128
    pack = jnp.pad(pack, ((0, 0), (0, 0), (0, packed - pack.shape[2])))
    by_partner = unxor([pack[j] for j in range(n_z)], z)
    out_t = output_w.T
    by_partner = [jnp.concatenate([v, out_t], axis=1) for v in by_partner]
    gathered = jnp.stack(unxor([swap_z(by_partner[k], k) for k in range(n_z)], z))

    x_own = tokens.reshape(tok, width)
    upward = [(i, i + n_y) for i in range(n_seq - n_y)]
    downward = [(i + n_y, i) for i in range(n_seq - n_y)]
    below, above = [x_own], [x_own]
    for _ in range(n_z - 1):
        below.append(lax.ppermute(below[-1], "seq", upward))
        above.append(lax.ppermute(above[-1], "seq", downward))
    x_parts = [x_own]
    for k in range(1, n_z):
        chosen = x_own
        for j in range(n_z):
            source = j ^ k
            value = below[j - source] if source < j else above[source - j]
            chosen = jnp.where(z == j, value, chosen)
        x_parts.append(chosen)

    for bit in y_bits:
        gathered = grow(gathered, "seq", bit, (y & bit) != 0)
    route_ids = routes.reshape(tok)
    choose = route_ids[:, None] == jnp.arange(experts, dtype=jnp.int32)[None, :]
    choose_f = choose.astype(f32)
    before = jnp.arange(tok)[:, None] > jnp.arange(tok)[None, :]
    earlier = dot_nn(before.astype(bf16), choose.astype(bf16))
    slot = jnp.sum(earlier * choose_f, axis=1).astype(jnp.int32)
    place = (route_ids ^ dp) * capacity + slot
    place_hot = jnp.arange(experts * capacity, dtype=jnp.int32)[:, None] == place[None, :]
    place_b = place_hot.astype(bf16)

    def to_experts(values):
        sent = dot_nn(place_b, values).astype(bf16).reshape(experts, capacity, -1)
        return [swap_dp(sent[k], k) for k in range(n_dp)]

    def weigh(values, rows):
        gates = rows[:, width : width + 1].astype(f32) + rows[:, width + 1 : width + 2].astype(f32)
        return (values.astype(f32) * gates).astype(bf16)

    def to_others(parts, *others):
        moved = [swap_y(v, k) for k in range(1, n_y) for v in parts]
        return jnp.concatenate([after(v, *others) for v in moved], axis=0)

    def from_experts(total):
        blocks = total.astype(bf16).reshape(n_dp, capacity, width)
        back = [swap_dp(blocks[k], k) for k in range(n_dp)]
        return dot_tn(place_b, jnp.concatenate(back, axis=0))

    def add_others(own, values):
        split = values.reshape(n_y - 1, n_dp * capacity, width)
        for k in range(1, n_y):
            own = own + swap_y(split[k - 1], k).astype(f32)
        return own

    upstream_b = cotangent.reshape(tok, width)
    upstream = upstream_b.astype(f32)

    for bit in reversed(dp_bits):
        gathered = grow(gathered, "dp", bit, (dp & bit) != 0)
    n_bits, m_bits = len(y_bits), len(dp_bits)
    order = tuple(reversed(range(m_bits))) + (m_bits + n_bits,)
    order = order + tuple(range(m_bits, m_bits + n_bits)) + (m_bits + n_bits + 1, m_bits + n_bits + 2)
    gathered = gathered.transpose(order).reshape(width, packed + inner)
    out_t = gathered[:, packed:]
    w_qkv = gathered[:, : 3 * part]
    gain_a = gathered[:, 3 * part].astype(f32)
    gain_f = gathered[:, 3 * part + 1].astype(f32)
    w_router = gathered[:, 3 * part + 2 : 3 * part + 2 + experts]
    table = gathered.reshape(n_dp, n_seq, w_rows, packed + inner)[0, :, :table_rows, table_at : table_at + heads]
    table = table.reshape(buckets, heads)

    z_groups = [[j * n_y + i for j in range(n_z)] for i in range(n_y)]
    up_down = jnp.stack([expert_in[0], expert_out[0]])
    x_all, up_down = lax.optimization_barrier((jnp.concatenate(x_parts, axis=0), up_down))
    up_down = lax.all_gather(up_down, "seq", axis=0, axis_index_groups=z_groups)

    x_all = x_all.astype(f32)
    scale_all = lax.rsqrt(jnp.mean(x_all * x_all, axis=-1, keepdims=True) + epsilon)
    normed_all = (x_all * scale_all * gain_a).astype(bf16)
    kv = dot_nn(normed_all, w_qkv[:, part:]).astype(bf16)
    kvs = [swap_y(kv, k) for k in range(n_y)]
    q = dot_nn(normed_all, w_qkv[:, :part]).astype(bf16)
    d_rows = to_experts(after(upstream_b, x_all))
    span = 2 * n_seq * local_len
    bucket_pad = jnp.concatenate([rel_bucket, jnp.full((1,), -1, jnp.int32)])
    bucket_hot = bucket_pad[None, :] == jnp.arange(buckets, dtype=jnp.int32)[:, None]
    table_pad = jnp.pad(table, ((0, 0), (0, 8 - heads)))
    vec = dot_tn(table_pad, bucket_hot.astype(bf16))
    pos = jnp.stack([z, y]).astype(jnp.int32)
    others = tuple(range(1, n_y))
    shape = (dims, seq_count, heads, size)
    before = attn_fwd(*shape, (0,), pos, vec, q, kvs[:1])
    d_rows = [after(v, *before) for v in d_rows]
    d_own = jnp.concatenate(d_rows, axis=0)
    context_parts, context_f = attn_fwd(*shape, others, pos, vec, q, kvs[1:], before)
    d_other = to_others(d_rows, context_parts)
    context_parts = context_parts.reshape(n_z, tok, part)
    context = [swap_z(context_parts[k], k) for k in range(n_z)]
    context = jnp.concatenate(unxor(context, z), axis=1)

    inputs = x_own.astype(f32)
    hidden_attn = inputs + dot_nt(context, out_t)
    scale_f = lax.rsqrt(jnp.mean(hidden_attn * hidden_attn, axis=-1, keepdims=True) + epsilon)
    normed_f = (hidden_attn * scale_f * gain_f).astype(bf16)
    logits = dot_nn(normed_f, w_router)
    router_p = jax.nn.softmax(logits, axis=-1)
    gate = jnp.sum(router_p * choose_f, axis=-1)

    gate_high = gate.astype(bf16)
    gate_low = (gate - gate_high.astype(f32)).astype(bf16)
    b_gate = jnp.stack([gate_high, gate_low], axis=1)
    b_gate = jnp.pad(b_gate, ((0, 0), (0, 126)))
    b_rows = to_experts(jnp.concatenate([normed_f, b_gate], axis=1))
    b_own = jnp.concatenate(b_rows, axis=0)
    dy_own = weigh(d_own, b_own)
    y_own, db_own, g_own, du_own = expert_call(
        expert_own_kernel, "expert_own", (b_own, dy_own), (), up_down, f32, 2
    )
    b_other = to_others(b_rows, y_own)
    dy_other = weigh(d_other, b_other)
    y_other, g_other, slope = expert_call(
        expert_fwd_kernel, "expert_fwd", (b_other,), (), up_down, bf16, 1
    )
    y_total = add_others(y_own, y_other)
    db_other, du_other = expert_call(
        expert_bwd_kernel, "expert_bwd", (dy_other,), (slope,), up_down, bf16, 1
    )
    db_total = add_others(db_own, db_other)
    y_total, b_late, dy_late = lax.optimization_barrier((y_total, b_other, dy_other))
    expert_tok = from_experts(y_total)
    grad_normed = from_experts(db_total)
    grad_up_down = expert_grad(
        (b_own, b_late, dy_own, dy_late), (du_own, du_other, g_own, g_other)
    )
    grad_up_down = lax.psum_scatter(
        grad_up_down, "seq", scatter_dimension=0, axis_index_groups=z_groups, tiled=True
    )
    grad_up = grad_up_down[:, 0].astype(f32)
    grad_down = grad_up_down[:, 1].astype(f32)

    mixed = (hidden_attn + gate[:, None] * expert_tok).astype(bf16).reshape(tokens.shape)
    grad_gate = jnp.sum(upstream * expert_tok, axis=-1)
    grad_logits = grad_gate[:, None] * router_p * (choose_f - gate[:, None])
    grad_router = lax.dot_general(
        normed_f.astype(f32), grad_logits, (((0,), (0,)), ((), ())), precision=highest
    )
    grad_normed = grad_normed + lax.dot_general(
        grad_logits, w_router.astype(f32), (((1,), (1,)), ((), ())), precision=highest
    )
    scaled = gain_f * grad_normed
    grad_hidden = upstream + scale_f * scaled
    grad_hidden = grad_hidden - hidden_attn * scale_f**3 * jnp.mean(
        scaled * hidden_attn, axis=-1, keepdims=True
    )
    grad_gain_f = jnp.sum(grad_normed * hidden_attn * scale_f, axis=0)
    grad_attn = grad_hidden.astype(bf16)

    grad_ctx = dot_nn(grad_attn, out_t).astype(bf16)
    grad_ctx = unxor([grad_ctx[:, j * part : (j + 1) * part] for j in range(n_z)], z)
    grad_ctx = jnp.concatenate([swap_z(grad_ctx[k], k) for k in range(n_z)], axis=0)
    grad_q, diag, *grad_kvs = attn_bwd(
        *shape, others, pos, vec, q, grad_ctx, context_f, kvs[1:]
    )
    arrived = [swap_y(grad_kvs[k - 1], k) for k in range(1, n_y)]
    grad_q, diag, grad_kv = attn_bwd(
        *shape, (0,), pos, vec, q, grad_ctx, context_f, kvs[:1], (grad_q, diag)
    )
    for value in arrived:
        grad_kv = grad_kv + value.astype(f32)
    grad_qkv = jnp.concatenate([grad_q, grad_kv.astype(bf16)], axis=1)
    grad_a_part = dot_nt(grad_qkv, w_qkv)
    grad_a_parts = grad_a_part.reshape(n_z, tok, width)
    grad_a_in = [swap_z(grad_a_parts[k].astype(bf16), k) for k in range(1, n_z)]

    grad_gain_a = jnp.sum(grad_a_part * x_all * scale_all, axis=0)
    diag = jnp.roll(diag, local_len - 1, axis=1)
    grad_table = lax.dot_general(
        diag, bucket_hot.astype(f32), (((1,), (1,)), ((), ())), precision=highest
    )
    grad_table = grad_table[:heads].T.reshape(1, n_seq, table_rows, heads)
    grad_table = jnp.pad(grad_table, ((0, 0), (0, 0), (0, w_rows - table_rows), (0, 0)))
    grad_table = jnp.broadcast_to(grad_table, (n_dp, n_seq, w_rows, heads)).reshape(width, heads)
    small = [grad_gain_a[:, None], grad_gain_f[:, None], grad_router, grad_table]
    small = jnp.concatenate(small, axis=1)
    small = jnp.pad(small, ((0, 0), (0, packed - 3 * part - small.shape[1])))
    value = weight_grad(normed_all, grad_qkv, grad_attn, context, small)
    value = after(value, grad_a_in[0])
    value = value.reshape((2,) * m_bits + (n_z,) + (2,) * n_bits + (w_rows, packed + inner))
    for i, bit in enumerate(dp_bits):
        value = halve(value, m_bits - 1 - i, "dp", bit, (dp & bit) != 0)
    value = after(value, *grad_a_in)
    value = after(value, grad_up_down)
    for i, bit in enumerate(y_bits):
        value = halve(value, n_bits - i, "seq", bit, (y & bit) != 0)
    parts = unxor([value[j] for j in range(n_z)], z)
    summed = unxor([swap_z(parts[k], k) for k in range(n_z)], z)
    grad_query, grad_key, grad_value = (
        jnp.concatenate([v[:, i * part : (i + 1) * part] for v in summed], axis=1).astype(f32)
        for i in range(3)
    )
    total = sum(v[:, 3 * part :].astype(f32) for v in summed)
    grad_gain_attn = total[:, 0]
    grad_gain_ffn = total[:, 1]
    grad_router = total[:, 2 : 2 + experts]
    grad_output = total[:, packed - 3 * part :].T
    grad_table = jnp.concatenate(
        [v[:table_rows, table_at : table_at + heads] for v in summed], axis=1
    ).astype(f32)

    grad_a = grad_a_parts[0]
    grad_a, grad_output = lax.optimization_barrier((grad_a, grad_output))
    for value in grad_a_in:
        grad_a = grad_a + value.astype(f32)
    scale_a = scale_all[:tok]
    scaled_a = gain_a * grad_a
    grad_x = grad_hidden + scale_a * scaled_a
    grad_x = grad_x - inputs * scale_a**3 * jnp.mean(scaled_a * inputs, axis=-1, keepdims=True)
    grad_tokens = grad_x.reshape(tokens.shape)

    return (
        mixed,
        grad_tokens,
        grad_gain_attn,
        grad_query,
        grad_key,
        grad_value,
        grad_output,
        grad_table,
        grad_gain_ffn,
        grad_router,
        grad_up,
        grad_down,
    )


def solution(mesh):
    vector = P(("dp", "seq"))
    matrix = P(("dp", "seq"), None)
    rows = P("dp", "seq", None)
    expert = P("dp", None, "seq")
    last = P(None, ("dp", "seq"))
    table = P("seq", None)
    return jax.shard_map(
        local,
        mesh=mesh,
        in_specs=(
            rows,
            rows,
            vector,
            matrix,
            matrix,
            matrix,
            last,
            table,
            P(),
            vector,
            matrix,
            P("dp", "seq", None, None),
            expert,
            expert,
        ),
        out_specs=(
            rows,
            rows,
            vector,
            matrix,
            matrix,
            matrix,
            last,
            table,
            vector,
            matrix,
            expert,
            expert,
        ),
        check_vma=False,
    )
```

```python
import math
from functools import partial

import jax
import jax.numpy as jnp
from jax import lax
from jax.experimental import pallas as pl
from jax.experimental.pallas import tpu as pltpu
from jax.sharding import PartitionSpec as P

epsilon = 1e-06
highest = lax.Precision.HIGHEST
bf16 = jnp.bfloat16
f32 = jnp.float32
VMEM = 56 * 1024 * 1024


def effort(flops):
    return pl.CostEstimate(flops=int(flops), transcendentals=0, bytes_accessed=int(flops) // 320)


def dot_nn(left, right):
    return lax.dot_general(left, right, (((1,), (0,)), ((), ())), preferred_element_type=f32)


def dot_tn(left, right):
    return lax.dot_general(left, right, (((0,), (0,)), ((), ())), preferred_element_type=f32)


def dot_nt(left, right):
    return lax.dot_general(left, right, (((1,), (1,)), ((), ())), preferred_element_type=f32)


def swap(value, axis, mask):
    size = lax.axis_size(axis)
    return lax.ppermute(value, axis, [(i, i ^ mask) for i in range(size)])


def bits_of(size):
    return [1 << i for i in range(size.bit_length() - 1)]


def unxor(parts, index):
    for bit in bits_of(len(parts)):
        flag = (index & bit) != 0
        parts = [jnp.where(flag, parts[j ^ bit], parts[j]) for j in range(len(parts))]
    return parts


def after(value, *others):
    return lax.optimization_barrier((value, *others))[0]


def grow(value, axis, mask, bit_set):
    other = swap(value, axis, mask)
    return jnp.stack([jnp.where(bit_set, other, value), jnp.where(bit_set, value, other)])


def pick(value, position, flag):
    low = lax.index_in_dim(value, 0, position, keepdims=False)
    high = lax.index_in_dim(value, 1, position, keepdims=False)
    return jnp.where(flag, high, low)


def halve(value, position, axis, mask, bit_set):
    sent = pick(value, position, jnp.logical_not(bit_set))
    kept = pick(value, position, bit_set)
    got = swap(sent, axis, mask)
    return (kept.astype(f32) + got.astype(f32)).astype(bf16)


def bias_tile(vec_ref, tile_ref, head):
    rows, width = tile_ref.shape
    vec = jnp.broadcast_to(vec_ref[pl.ds(head, 1), :], (rows, width))
    tile_ref[...] = pltpu.roll(vec, width - (rows - 1), 1, stride=1, stride_axis=0)


def key_columns(pos_ref, dims, key_ys, query_z):
    n_z, n_y, local_len = dims
    z, y = pos_ref[0], pos_ref[1]
    query_block = (z ^ query_z) * n_y + y
    columns = []
    for key_y in key_ys:
        for key_z in range(n_z):
            key_block = (z ^ key_z) * n_y + (y ^ key_y)
            first = (n_z * n_y - 1 - query_block + key_block) * local_len
            columns.append(pl.ds(pl.multiple_of(first, local_len), local_len))
    return columns


def split_keys(dims, seq_count, heads, size, kv_refs, offset, plain_ref, turned_ref):
    n_z, _, local_len = dims
    for head in range(heads):
        lo, hi = offset + head * size, offset + (head + 1) * size
        for s in range(seq_count):
            index = head * seq_count + s
            for group, kv_ref in enumerate(kv_refs):
                for key_z in range(n_z):
                    at = (key_z * seq_count + s) * local_len
                    to = (group * n_z + key_z) * local_len
                    block = kv_ref[at : at + local_len, lo:hi]
                    if plain_ref is not None:
                        plain_ref[index, to : to + local_len, :] = block
                    if turned_ref is not None:
                        turned_ref[index, :, to : to + local_len] = block.T


def attn_fwd_kernel(dims, seq_count, heads, size, key_ys, first, pos_ref, vec_ref, q_ref, *refs):
    n_z, _, local_len = dims
    kv_refs, refs = refs[: len(key_ys)], refs[len(key_ys) :]
    if first:
        out_ref, *refs = refs
    else:
        out_in, c_ref, out_ref, *refs = refs
    tile_ref, kt_ref, v_ref, qh_ref = refs
    inner = heads * size
    split_keys(dims, seq_count, heads, size, kv_refs, 0, None, kt_ref)
    split_keys(dims, seq_count, heads, size, kv_refs, inner, v_ref, None)
    for head in range(heads):
        qh_ref[head] = q_ref[:, head * size : (head + 1) * size]

    def head_step(head, carry):
        bias_tile(vec_ref, tile_ref, head)

        def query_step(query_z, carry):
            columns = key_columns(pos_ref, dims, key_ys, query_z)
            for s in range(seq_count):
                row = pl.multiple_of((query_z * seq_count + s) * local_len, local_len)
                rows = pl.ds(row, local_len)
                bias = jnp.concatenate([tile_ref[:, c] for c in columns], axis=1)
                score = dot_nn(qh_ref[head, rows, :], kt_ref[head * seq_count + s]) + bias
                top = jnp.max(score, axis=1, keepdims=True)
                if not first:
                    top_before = out_in[head, rows, size : size + 1]
                    top = jnp.maximum(top, top_before)
                weight = jnp.exp(score - top)
                total = jnp.sum(weight, axis=1, keepdims=True)
                out = dot_nn(weight.astype(bf16), v_ref[head * seq_count + s])
                if first:
                    out_ref[head, rows, :size] = out
                    out_ref[head, rows, size : size + 1] = top
                    out_ref[head, rows, size + 1 : size + 2] = total
                else:
                    fade = jnp.exp(top_before - top)
                    total = total + fade * out_in[head, rows, size + 1 : size + 2]
                    out_ref[head, rows, :size] = (out + fade * out_in[head, rows, :size]) / total
                    out_ref[head, rows, size : size + 1] = top + jnp.log(total)
            return carry

        return lax.fori_loop(0, n_z, query_step, carry, unroll=2)

    lax.fori_loop(0, heads, head_step, 0)
    if not first:
        for head in range(heads):
            c_ref[:, head * size : (head + 1) * size] = out_ref[head, :, :size].astype(bf16)


def attn_bwd_kernel(dims, seq_count, heads, size, key_ys, first, pos_ref, vec_ref, q_ref, *refs):
    n_z, _, local_len = dims
    count = len(key_ys)
    dc_ref, c_ref, *refs = refs
    kv_refs, refs = refs[:count], refs[count:]
    if first:
        dq_ref, diag_ref, *refs = refs
        dqh_ref = dq_ref
    else:
        dq_in, diag_in, dq_ref, diag_ref, *refs = refs
    dkv_refs, refs = refs[:count], refs[count:]
    tile_ref, grad_ref, kt_ref, vt_ref, k_ref, qh_ref, dch_ref, delta_ref, dk_ref, dv_ref = refs[:10]
    if not first:
        dqh_ref = refs[10]
    inner = heads * size
    split_keys(dims, seq_count, heads, size, kv_refs, 0, k_ref, kt_ref)
    split_keys(dims, seq_count, heads, size, kv_refs, inner, None, vt_ref)
    for head in range(heads):
        qh_ref[head] = q_ref[:, head * size : (head + 1) * size]
        dc = dc_ref[:, head * size : (head + 1) * size]
        dch_ref[head] = dc
        delta_ref[head] = jnp.sum(dc.astype(f32) * c_ref[head, :, :size], axis=1, keepdims=True)
    if first:
        diag_ref[...] = jnp.zeros_like(diag_ref)
    else:
        diag_ref[...] = diag_in[...]
    dk_ref[...] = jnp.zeros_like(dk_ref)
    dv_ref[...] = jnp.zeros_like(dv_ref)

    def head_step(head, carry):
        bias_tile(vec_ref, tile_ref, head)
        grad_ref[...] = jnp.zeros_like(grad_ref)

        def query_step(query_z, carry):
            columns = key_columns(pos_ref, dims, key_ys, query_z)
            for s in range(seq_count):
                index = head * seq_count + s
                row = pl.multiple_of((query_z * seq_count + s) * local_len, local_len)
                rows = pl.ds(row, local_len)
                q = qh_ref[head, rows, :]
                dc = dch_ref[head, rows, :]
                bias = jnp.concatenate([tile_ref[:, c] for c in columns], axis=1)
                prob = jnp.exp(dot_nn(q, kt_ref[index]) + bias - c_ref[head, rows, size : size + 1])
                dprob = dot_nn(dc, vt_ref[index])
                ds_f = prob * (dprob - delta_ref[head, rows, :])
                ds = ds_f.astype(bf16)
                dq = dot_nn(ds, k_ref[index])
                if not first:
                    dq = dq + dq_in[head, rows, :]
                dqh_ref[head, rows, :] = dq
                dk_ref[index] += dot_tn(q, ds)
                dv_ref[index] += dot_tn(dc, prob.astype(bf16))
                for i, c in enumerate(columns):
                    grad_ref[:, c] += ds_f[:, i * local_len : (i + 1) * local_len]
            return carry

        lax.fori_loop(0, n_z, query_step, 0, unroll=2)
        folded = grad_ref[...]
        width = folded.shape[1]
        while folded.shape[0] > 1:
            half = folded.shape[0] // 2
            folded = folded[:half] + pltpu.roll(folded[half:], width - half, 1)
        diag_ref[pl.ds(head, 1), :] += folded
        return carry

    lax.fori_loop(0, heads, head_step, 0)
    for head in range(heads):
        lo, hi = head * size, (head + 1) * size
        if not first:
            dq_ref[:, lo:hi] = dqh_ref[head].astype(bf16)
        for s in range(seq_count):
            index = head * seq_count + s
            for group, out in enumerate(dkv_refs):
                for key_z in range(n_z):
                    at = (key_z * seq_count + s) * local_len
                    to = (group * n_z + key_z) * local_len
                    cut = slice(to, to + local_len)
                    out[at : at + local_len, lo:hi] = dk_ref[index, :, cut].T.astype(out.dtype)
                    out[at : at + local_len, inner + lo : inner + hi] = dv_ref[
                        index, :, cut
                    ].T.astype(out.dtype)


def vmem_specs(count):
    return [pl.BlockSpec(memory_space=pltpu.VMEM) for _ in range(count)]


def attn_fwd(dims, seq_count, heads, size, key_ys, pos, vec, q, kvs, before=()):
    rows = q.shape[0]
    length = len(key_ys) * dims[0] * dims[2]
    both = heads * seq_count
    first = not before
    wide = jax.ShapeDtypeStruct((heads, rows, 2 * size), f32)
    joined = jax.ShapeDtypeStruct((rows, heads * size), bf16)
    return pl.pallas_call(
        partial(attn_fwd_kernel, dims, seq_count, heads, size, key_ys, first),
        out_shape=(wide,) if first else (joined, wide),
        in_specs=[pl.BlockSpec(memory_space=pltpu.SMEM)]
        + vmem_specs(2 + len(kvs) + len(before)),
        out_specs=tuple(vmem_specs(1 if first else 2)),
        scratch_shapes=[
            pltpu.VMEM((dims[2], vec.shape[1]), f32),
            pltpu.VMEM((both, size, length), bf16),
            pltpu.VMEM((both, length, size), bf16),
            pltpu.VMEM((heads, rows, size), bf16),
        ],
        compiler_params=pltpu.CompilerParams(vmem_limit_bytes=VMEM),
        cost_estimate=effort(5000 * heads * rows * length),
        name="attn_fwd",
    )(pos, vec, q, *kvs, *before)


def attn_bwd(dims, seq_count, heads, size, key_ys, pos, vec, q, dc, c, kvs, before=()):
    rows = q.shape[0]
    length = len(key_ys) * dims[0] * dims[2]
    both = heads * seq_count
    first = not before
    wide = jax.ShapeDtypeStruct((heads, rows, size), f32)
    joined = jax.ShapeDtypeStruct((rows, heads * size), bf16)
    shapes = [wide if first else joined, jax.ShapeDtypeStruct(vec.shape, f32)]
    for key_y in key_ys:
        shapes.append(jax.ShapeDtypeStruct(kvs[0].shape, bf16 if key_y else f32))
    scratch = [
        pltpu.VMEM((dims[2], vec.shape[1]), f32),
        pltpu.VMEM((dims[2], vec.shape[1]), f32),
        pltpu.VMEM((both, size, length), bf16),
        pltpu.VMEM((both, size, length), bf16),
        pltpu.VMEM((both, length, size), bf16),
        pltpu.VMEM((heads, rows, size), bf16),
        pltpu.VMEM((heads, rows, size), bf16),
        pltpu.VMEM((heads, rows, 1), f32),
        pltpu.VMEM((both, size, length), f32),
        pltpu.VMEM((both, size, length), f32),
    ]
    if not first:
        scratch.append(pltpu.VMEM((heads, rows, size), f32))
    return pl.pallas_call(
        partial(attn_bwd_kernel, dims, seq_count, heads, size, key_ys, first),
        out_shape=tuple(shapes),
        in_specs=[pl.BlockSpec(memory_space=pltpu.SMEM)]
        + vmem_specs(4 + len(kvs) + len(before)),
        out_specs=tuple(vmem_specs(len(shapes))),
        scratch_shapes=scratch,
        compiler_params=pltpu.CompilerParams(vmem_limit_bytes=VMEM),
        cost_estimate=effort(7500 * heads * rows * length),
        name="attn_bwd",
    )(pos, vec, q, dc, c, *kvs, *before)


def gelu_parts(pre):
    square = pre * pre
    tanh = jnp.tanh(0.7978845608028654 * (pre + 0.044715 * pre * square))
    hidden = 0.5 * pre * (1.0 + tanh)
    slope = 0.5 * (1.0 + tanh) + 0.5 * pre * (1.0 - tanh * tanh) * (
        0.7978845608028654 * (1.0 + 0.134145 * square)
    )
    return hidden.astype(bf16), slope


def accumulate(out_ref, acc_ref, value):
    step = pl.program_id(0)

    @pl.when(step == 0)
    def _():
        acc_ref[...] = value

    @pl.when(step > 0)
    def _():
        acc_ref[...] += value

    @pl.when(step == pl.num_programs(0) - 1)
    def _():
        out_ref[...] = acc_ref[...].astype(out_ref.dtype)


def expert_own_kernel(rows_ref, dy_ref, weight_ref, y_ref, db_ref, g_ref, du_ref, y_acc, db_acc):
    hidden, slope = gelu_parts(dot_nn(rows_ref[...], weight_ref[0, 0]))
    g_ref[0] = hidden
    accumulate(y_ref, y_acc, dot_nt(hidden, weight_ref[0, 1]))
    du = (dot_nn(dy_ref[...], weight_ref[0, 1]) * slope).astype(bf16)
    du_ref[0] = du
    accumulate(db_ref, db_acc, dot_nt(du, weight_ref[0, 0]))


def expert_fwd_kernel(rows_ref, weight_ref, y_ref, g_ref, slope_ref, y_acc):
    hidden, slope = gelu_parts(dot_nn(rows_ref[...], weight_ref[0, 0]))
    g_ref[0] = hidden
    slope_ref[0] = slope.astype(bf16)
    accumulate(y_ref, y_acc, dot_nt(hidden, weight_ref[0, 1]))


def expert_bwd_kernel(dy_ref, slope_ref, weight_ref, db_ref, du_ref, db_acc):
    du = (dot_nn(dy_ref[...], weight_ref[0, 1]) * slope_ref[0].astype(f32)).astype(bf16)
    du_ref[0] = du
    accumulate(db_ref, db_acc, dot_nt(du, weight_ref[0, 0]))


def expert_call(kernel, name, rows, kept_in, up_down, out_type, wholes):
    count = rows[0].shape[0]
    n_z, _, width, hidden = up_down.shape
    whole = pl.BlockSpec((count, width), lambda i: (0, 0))
    weight = pl.BlockSpec((1, 2, width, hidden), lambda i: (i, 0, 0, 0))
    kept = pl.BlockSpec((1, count, hidden), lambda i: (i, 0, 0))
    kept_out = 1 if kept_in else 2
    return pl.pallas_call(
        kernel,
        grid=(n_z,),
        out_shape=(jax.ShapeDtypeStruct((count, width), out_type),) * wholes
        + (jax.ShapeDtypeStruct((n_z, count, hidden), bf16),) * kept_out,
        in_specs=[whole] * len(rows) + [kept] * len(kept_in) + [weight],
        out_specs=(whole,) * wholes + (kept,) * kept_out,
        scratch_shapes=[pltpu.VMEM((count, width), f32)] * wholes,
        compiler_params=pltpu.CompilerParams(vmem_limit_bytes=VMEM),
        cost_estimate=effort(12 * count * width * hidden * n_z * wholes),
        name=name,
    )(*rows, *kept_in, up_down)


def expert_grad_kernel(b_ref, b_other, dy_ref, dy_other, du_ref, du_other, g_ref, g_other, out_ref):
    grad_up = dot_tn(b_ref[...], du_ref[0]) + dot_tn(b_other[...], du_other[0])
    out_ref[0, 0] = grad_up.astype(bf16)
    grad_down = dot_tn(dy_ref[...], g_ref[0]) + dot_tn(dy_other[...], g_other[0])
    out_ref[0, 1] = grad_down.astype(bf16)


def expert_grad(rows, kept):
    width = rows[2].shape[1]
    n_z, _, hidden = kept[0].shape
    return pl.pallas_call(
        expert_grad_kernel,
        grid=(n_z,),
        out_shape=jax.ShapeDtypeStruct((n_z, 2, width, hidden), bf16),
        in_specs=[pl.BlockSpec((v.shape[0], width), lambda i: (0, 0)) for v in rows]
        + [pl.BlockSpec((1,) + v.shape[1:], lambda i: (i, 0, 0)) for v in kept],
        out_specs=pl.BlockSpec((1, 2, width, hidden), lambda i: (i, 0, 0, 0)),
        compiler_params=pltpu.CompilerParams(vmem_limit_bytes=VMEM),
        cost_estimate=effort(5 * 2 * sum(v.shape[0] for v in rows) * width * hidden * n_z),
        name="expert_grad",
    )(*rows, *kept)


def weight_grad_kernel(a_ref, grad_ref, out_grad_ref, context_ref, small_ref, out_ref):
    cut = grad_ref.shape[1]
    wide = cut + small_ref.shape[1]
    out_ref[:, :cut] = dot_tn(a_ref[...], grad_ref[...]).astype(bf16)
    out_ref[:, cut:wide] = small_ref[...].astype(bf16)
    out_ref[:, wide:] = dot_tn(out_grad_ref[...], context_ref[...]).astype(bf16)


def weight_grad(a, grad, out_grad, context, small):
    width = a.shape[1]
    columns = grad.shape[1] + small.shape[1] + context.shape[1]
    return pl.pallas_call(
        weight_grad_kernel,
        out_shape=jax.ShapeDtypeStruct((width, columns), bf16),
        in_specs=vmem_specs(5),
        out_specs=vmem_specs(1)[0],
        compiler_params=pltpu.CompilerParams(vmem_limit_bytes=VMEM),
        cost_estimate=effort(4 * 2 * a.shape[0] * width * columns),
        name="weight_grad",
    )(a, grad, out_grad, context, small)


def local(
    tokens,
    cotangent,
    gain_attn,
    query_w,
    key_w,
    value_w,
    output_w,
    rel_table,
    rel_bucket,
    gain_ffn,
    router_w,
    routes,
    expert_in,
    expert_out,
):
    seq_count, local_len, width = tokens.shape
    tok = seq_count * local_len
    n_dp, n_seq = lax.axis_size("dp"), lax.axis_size("seq")
    head_count = rel_table.shape[1]
    inner = query_w.shape[1]
    size = inner // head_count
    n_z = math.gcd(head_count, n_seq)
    n_y = n_seq // n_z
    heads = head_count // n_z
    part = heads * size
    experts = router_w.shape[1]
    capacity = 2 * tok // experts
    table_rows = rel_table.shape[0]
    buckets = table_rows * n_seq
    w_rows = query_w.shape[0]
    dims = (n_z, n_y, local_len)
    dp, seq = lax.axis_index("dp"), lax.axis_index("seq")
    z, y = seq // n_y, seq % n_y
    dp_bits, y_bits, z_bits = bits_of(n_dp), bits_of(n_y), bits_of(n_z)

    def swap_z(value, k):
        return swap(value, "seq", k * n_y) if k else value

    def swap_y(value, k):
        return swap(value, "seq", k) if k else value

    def swap_dp(value, k):
        return swap(value, "dp", k) if k else value

    extra = jnp.concatenate([gain_attn[:, None], gain_ffn[:, None], router_w], axis=1)
    extra = jnp.broadcast_to(extra[None], (n_z, w_rows, 2 + experts))
    table_at = part * 3 + 2 + experts
    table = rel_table.reshape(table_rows, n_z, heads).transpose(1, 0, 2)
    table = jnp.pad(table, ((0, 0), (0, w_rows - table_rows), (0, 0)))
    joined = [w.reshape(w_rows, n_z, part).transpose(1, 0, 2) for w in (query_w, key_w, value_w)]
    pack = jnp.concatenate(joined + [extra, table], axis=2)
    packed = -(-pack.shape[2] // 128) * 128
    pack = jnp.pad(pack, ((0, 0), (0, 0), (0, packed - pack.shape[2])))
    by_partner = unxor([pack[j] for j in range(n_z)], z)
    out_t = output_w.T
    by_partner = [jnp.concatenate([v, out_t], axis=1) for v in by_partner]
    gathered = jnp.stack(unxor([swap_z(by_partner[k], k) for k in range(n_z)], z))

    x_own = tokens.reshape(tok, width)
    upward = [(i, i + n_y) for i in range(n_seq - n_y)]
    downward = [(i + n_y, i) for i in range(n_seq - n_y)]
    below, above = [x_own], [x_own]
    for _ in range(n_z - 1):
        below.append(lax.ppermute(below[-1], "seq", upward))
        above.append(lax.ppermute(above[-1], "seq", downward))
    x_parts = [x_own]
    for k in range(1, n_z):
        chosen = x_own
        for j in range(n_z):
            source = j ^ k
            value = below[j - source] if source < j else above[source - j]
            chosen = jnp.where(z == j, value, chosen)
        x_parts.append(chosen)

    for bit in y_bits:
        gathered = grow(gathered, "seq", bit, (y & bit) != 0)
    route_ids = routes.reshape(tok)
    choose = route_ids[:, None] == jnp.arange(experts, dtype=jnp.int32)[None, :]
    choose_f = choose.astype(f32)
    before = jnp.arange(tok)[:, None] > jnp.arange(tok)[None, :]
    earlier = dot_nn(before.astype(bf16), choose.astype(bf16))
    slot = jnp.sum(earlier * choose_f, axis=1).astype(jnp.int32)
    place = (route_ids ^ dp) * capacity + slot
    place_hot = jnp.arange(experts * capacity, dtype=jnp.int32)[:, None] == place[None, :]
    place_b = place_hot.astype(bf16)

    def to_experts(values):
        sent = dot_nn(place_b, values).astype(bf16).reshape(experts, capacity, -1)
        return [swap_dp(sent[k], k) for k in range(n_dp)]

    def weigh(values, rows):
        gates = rows[:, width : width + 1].astype(f32) + rows[:, width + 1 : width + 2].astype(f32)
        return (values.astype(f32) * gates).astype(bf16)

    def to_others(parts, *others):
        moved = [swap_y(v, k) for k in range(1, n_y) for v in parts]
        return jnp.concatenate([after(v, *others) for v in moved], axis=0)

    def from_experts(total):
        blocks = total.astype(bf16).reshape(n_dp, capacity, width)
        back = [swap_dp(blocks[k], k) for k in range(n_dp)]
        return dot_tn(place_b, jnp.concatenate(back, axis=0))

    def add_others(own, values):
        split = values.reshape(n_y - 1, n_dp * capacity, width)
        for k in range(1, n_y):
            own = own + swap_y(split[k - 1], k).astype(f32)
        return own

    upstream_b = cotangent.reshape(tok, width)
    upstream = upstream_b.astype(f32)

    for bit in reversed(dp_bits):
        gathered = grow(gathered, "dp", bit, (dp & bit) != 0)
    n_bits, m_bits = len(y_bits), len(dp_bits)
    order = tuple(reversed(range(m_bits))) + (m_bits + n_bits,)
    order = order + tuple(range(m_bits, m_bits + n_bits)) + (m_bits + n_bits + 1, m_bits + n_bits + 2)
    gathered = gathered.transpose(order).reshape(width, packed + inner)
    out_t = gathered[:, packed:]
    w_qkv = gathered[:, : 3 * part]
    gain_a = gathered[:, 3 * part].astype(f32)
    gain_f = gathered[:, 3 * part + 1].astype(f32)
    w_router = gathered[:, 3 * part + 2 : 3 * part + 2 + experts]
    table = gathered.reshape(n_dp, n_seq, w_rows, packed + inner)[0, :, :table_rows, table_at : table_at + heads]
    table = table.reshape(buckets, heads)

    z_groups = [[j * n_y + i for j in range(n_z)] for i in range(n_y)]
    up_down = jnp.stack([expert_in[0], expert_out[0]])
    x_all, up_down = lax.optimization_barrier((jnp.concatenate(x_parts, axis=0), up_down))
    up_down = lax.all_gather(up_down, "seq", axis=0, axis_index_groups=z_groups)

    x_all = x_all.astype(f32)
    scale_all = lax.rsqrt(jnp.mean(x_all * x_all, axis=-1, keepdims=True) + epsilon)
    normed_all = (x_all * scale_all * gain_a).astype(bf16)
    kv = dot_nn(normed_all, w_qkv[:, part:]).astype(bf16)
    kvs = [swap_y(kv, k) for k in range(n_y)]
    q = dot_nn(normed_all, w_qkv[:, :part]).astype(bf16)
    d_rows = to_experts(after(upstream_b, x_all))
    span = 2 * n_seq * local_len
    bucket_pad = jnp.concatenate([rel_bucket, jnp.full((1,), -1, jnp.int32)])
    bucket_hot = bucket_pad[None, :] == jnp.arange(buckets, dtype=jnp.int32)[:, None]
    table_pad = jnp.pad(table, ((0, 0), (0, 8 - heads)))
    vec = dot_tn(table_pad, bucket_hot.astype(bf16))
    pos = jnp.stack([z, y]).astype(jnp.int32)
    others = tuple(range(1, n_y))
    shape = (dims, seq_count, heads, size)
    before = attn_fwd(*shape, (0,), pos, vec, q, kvs[:1])
    d_rows = [after(v, *before) for v in d_rows]
    d_own = jnp.concatenate(d_rows, axis=0)
    context_parts, context_f = attn_fwd(*shape, others, pos, vec, q, kvs[1:], before)
    d_other = to_others(d_rows, context_parts)
    context_parts = after(context_parts, *d_rows).reshape(n_z, tok, part)
    context = [swap_z(context_parts[k], k) for k in range(n_z)]
    context = jnp.concatenate(unxor(context, z), axis=1)

    inputs = x_own.astype(f32)
    hidden_attn = inputs + dot_nt(context, out_t)
    scale_f = lax.rsqrt(jnp.mean(hidden_attn * hidden_attn, axis=-1, keepdims=True) + epsilon)
    normed_f = (hidden_attn * scale_f * gain_f).astype(bf16)
    logits = dot_nn(normed_f, w_router)
    router_p = jax.nn.softmax(logits, axis=-1)
    gate = jnp.sum(router_p * choose_f, axis=-1)

    gate_high = gate.astype(bf16)
    gate_low = (gate - gate_high.astype(f32)).astype(bf16)
    b_gate = jnp.stack([gate_high, gate_low], axis=1)
    b_gate = jnp.pad(b_gate, ((0, 0), (0, 126)))
    b_rows = to_experts(jnp.concatenate([normed_f, b_gate], axis=1))
    b_own = jnp.concatenate(b_rows, axis=0)
    dy_own = weigh(d_own, b_own)
    y_own, db_own, g_own, du_own = expert_call(
        expert_own_kernel, "expert_own", (b_own, dy_own), (), up_down, f32, 2
    )
    b_other = to_others(b_rows, y_own)
    dy_other = weigh(d_other, b_other)
    y_other, g_other, slope = expert_call(
        expert_fwd_kernel, "expert_fwd", (b_other,), (), up_down, bf16, 1
    )
    y_total = add_others(y_own, y_other)
    db_other, du_other = expert_call(
        expert_bwd_kernel, "expert_bwd", (dy_other,), (slope,), up_down, bf16, 1
    )
    db_total = add_others(db_own, db_other)
    grad_up_down = expert_grad(
        (b_own, b_other, dy_own, dy_other), (du_own, du_other, g_own, g_other)
    )
    expert_tok = from_experts(after(y_total, grad_up_down))
    grad_normed = from_experts(db_total)
    grad_up_down = lax.psum_scatter(
        grad_up_down, "seq", scatter_dimension=0, axis_index_groups=z_groups, tiled=True
    )
    grad_up = grad_up_down[:, 0].astype(f32)
    grad_down = grad_up_down[:, 1].astype(f32)

    mixed = (hidden_attn + gate[:, None] * expert_tok).astype(bf16).reshape(tokens.shape)
    grad_gate = jnp.sum(upstream * expert_tok, axis=-1)
    grad_logits = grad_gate[:, None] * router_p * (choose_f - gate[:, None])
    grad_router = lax.dot_general(
        normed_f.astype(f32), grad_logits, (((0,), (0,)), ((), ())), precision=highest
    )
    grad_normed = grad_normed + lax.dot_general(
        grad_logits, w_router.astype(f32), (((1,), (1,)), ((), ())), precision=highest
    )
    scaled = gain_f * grad_normed
    grad_hidden = upstream + scale_f * scaled
    grad_hidden = grad_hidden - hidden_attn * scale_f**3 * jnp.mean(
        scaled * hidden_attn, axis=-1, keepdims=True
    )
    grad_gain_f = jnp.sum(grad_normed * hidden_attn * scale_f, axis=0)
    grad_attn = grad_hidden.astype(bf16)

    grad_ctx = dot_nn(grad_attn, out_t).astype(bf16)
    grad_ctx = unxor([grad_ctx[:, j * part : (j + 1) * part] for j in range(n_z)], z)
    grad_ctx = jnp.concatenate([swap_z(grad_ctx[k], k) for k in range(n_z)], axis=0)
    grad_q, diag, *grad_kvs = attn_bwd(
        *shape, others, pos, vec, q, grad_ctx, context_f, kvs[1:]
    )
    arrived = [swap_y(grad_kvs[k - 1], k) for k in range(1, n_y)]
    grad_q, diag, grad_kv = attn_bwd(
        *shape, (0,), pos, vec, q, grad_ctx, context_f, kvs[:1], (grad_q, diag)
    )
    for value in arrived:
        grad_kv = grad_kv + value.astype(f32)
    grad_qkv = jnp.concatenate([grad_q, grad_kv.astype(bf16)], axis=1)
    odd, even = list(range(1, n_z, 2)), list(range(0, n_z, 2))

    def take(value, blocks):
        value = value.reshape(n_z, tok, value.shape[1])
        return jnp.concatenate([value[k] for k in blocks], axis=0)

    sent = dot_nt(take(grad_qkv, odd), w_qkv)
    got = swap_z(sent.astype(bf16), 1)
    kept = dot_nt(take(grad_qkv, even), w_qkv)
    grad_gain_a = jnp.sum(sent * take(x_all * scale_all, odd), axis=0)
    grad_gain_a = grad_gain_a + jnp.sum(kept * take(x_all * scale_all, even), axis=0)
    diag = jnp.roll(diag, local_len - 1, axis=1)
    grad_table = lax.dot_general(
        diag, bucket_hot.astype(f32), (((1,), (1,)), ((), ())), precision=highest
    )
    grad_table = grad_table[:heads].T.reshape(1, n_seq, table_rows, heads)
    grad_table = jnp.pad(grad_table, ((0, 0), (0, 0), (0, w_rows - table_rows), (0, 0)))
    grad_table = jnp.broadcast_to(grad_table, (n_dp, n_seq, w_rows, heads)).reshape(width, heads)
    small = [grad_gain_a[:, None], grad_gain_f[:, None], grad_router, grad_table]
    small = jnp.concatenate(small, axis=1)
    small = jnp.pad(small, ((0, 0), (0, packed - 3 * part - small.shape[1])))
    value = weight_grad(normed_all, grad_qkv, grad_attn, context, small)
    value = value.reshape((2,) * m_bits + (n_z,) + (2,) * n_bits + (w_rows, packed + inner))
    for i, bit in enumerate(dp_bits):
        value = halve(value, m_bits - 1 - i, "dp", bit, (dp & bit) != 0)
    got = after(got, value)
    grad_a = (kept + got.astype(f32)).reshape(n_z // 2, tok, width)
    for bit in bits_of(n_z // 2):
        half = [k for k in range(0, grad_a.shape[0], 2)]
        far = jnp.concatenate([grad_a[k + 1] for k in half]).astype(bf16)
        far = swap_z(far, 2 * bit).astype(f32).reshape(len(half), tok, width)
        grad_a = jnp.stack([grad_a[k] for k in half]) + far
    for i, bit in enumerate(y_bits):
        value = halve(value, n_bits - i, "seq", bit, (y & bit) != 0)
    value = after(value, grad_up_down)
    parts = unxor([value[j] for j in range(n_z)], z)
    summed = unxor([swap_z(parts[k], k) for k in range(n_z)], z)
    grad_query, grad_key, grad_value = (
        jnp.concatenate([v[:, i * part : (i + 1) * part] for v in summed], axis=1).astype(f32)
        for i in range(3)
    )
    total = sum(v[:, 3 * part :].astype(f32) for v in summed)
    grad_gain_attn = total[:, 0]
    grad_gain_ffn = total[:, 1]
    grad_router = total[:, 2 : 2 + experts]
    grad_output = total[:, packed - 3 * part :].T
    grad_table = jnp.concatenate(
        [v[:table_rows, table_at : table_at + heads] for v in summed], axis=1
    ).astype(f32)

    grad_a = grad_a[0]
    scale_a = scale_all[:tok]
    scaled_a = gain_a * grad_a
    grad_x = grad_hidden + scale_a * scaled_a
    grad_x = grad_x - inputs * scale_a**3 * jnp.mean(scaled_a * inputs, axis=-1, keepdims=True)
    grad_tokens = grad_x.reshape(tokens.shape)

    return (
        mixed,
        grad_tokens,
        grad_gain_attn,
        grad_query,
        grad_key,
        grad_value,
        grad_output,
        grad_table,
        grad_gain_ffn,
        grad_router,
        grad_up,
        grad_down,
    )


def solution(mesh):
    vector = P(("dp", "seq"))
    matrix = P(("dp", "seq"), None)
    rows = P("dp", "seq", None)
    expert = P("dp", None, "seq")
    last = P(None, ("dp", "seq"))
    table = P("seq", None)
    return jax.shard_map(
        local,
        mesh=mesh,
        in_specs=(
            rows,
            rows,
            vector,
            matrix,
            matrix,
            matrix,
            last,
            table,
            P(),
            vector,
            matrix,
            P("dp", "seq", None, None),
            expert,
            expert,
        ),
        out_specs=(
            rows,
            rows,
            vector,
            matrix,
            matrix,
            matrix,
            last,
            table,
            vector,
            matrix,
            expert,
            expert,
        ),
        check_vma=False,
    )
```

```python
import math
from functools import partial

import jax
import jax.numpy as jnp
from jax import lax
from jax.experimental import pallas as pl
from jax.experimental.pallas import tpu as pltpu
from jax.sharding import PartitionSpec as P

epsilon = 1e-06
highest = lax.Precision.HIGHEST
bf16 = jnp.bfloat16
f32 = jnp.float32
VMEM = 56 * 1024 * 1024


def effort(flops):
    return pl.CostEstimate(flops=int(flops), transcendentals=0, bytes_accessed=int(flops) // 320)


def dot_nn(left, right):
    return lax.dot_general(left, right, (((1,), (0,)), ((), ())), preferred_element_type=f32)


def dot_tn(left, right):
    return lax.dot_general(left, right, (((0,), (0,)), ((), ())), preferred_element_type=f32)


def dot_nt(left, right):
    return lax.dot_general(left, right, (((1,), (1,)), ((), ())), preferred_element_type=f32)


def swap(value, axis, mask):
    size = lax.axis_size(axis)
    return lax.ppermute(value, axis, [(i, i ^ mask) for i in range(size)])


def bits_of(size):
    return [1 << i for i in range(size.bit_length() - 1)]


def unxor(parts, index):
    for bit in bits_of(len(parts)):
        flag = (index & bit) != 0
        parts = [jnp.where(flag, parts[j ^ bit], parts[j]) for j in range(len(parts))]
    return parts


def after(value, *others):
    return lax.optimization_barrier((value, *others))[0]


def grow(value, axis, mask, bit_set):
    other = swap(value, axis, mask)
    return jnp.stack([jnp.where(bit_set, other, value), jnp.where(bit_set, value, other)])


def pick(value, position, flag):
    low = lax.index_in_dim(value, 0, position, keepdims=False)
    high = lax.index_in_dim(value, 1, position, keepdims=False)
    return jnp.where(flag, high, low)


def halve(value, position, axis, mask, bit_set):
    sent = pick(value, position, jnp.logical_not(bit_set))
    kept = pick(value, position, bit_set)
    got = swap(sent, axis, mask)
    return (kept.astype(f32) + got.astype(f32)).astype(bf16)


def bias_tile(vec_ref, tile_ref, head):
    rows, width = tile_ref.shape
    vec = jnp.broadcast_to(vec_ref[pl.ds(head, 1), :], (rows, width))
    tile_ref[...] = pltpu.roll(vec, width - (rows - 1), 1, stride=1, stride_axis=0)


def key_columns(pos_ref, dims, key_ys, query_z):
    n_z, n_y, local_len = dims
    z, y = pos_ref[0], pos_ref[1]
    query_block = (z ^ query_z) * n_y + y
    columns = []
    for key_y in key_ys:
        for key_z in range(n_z):
            key_block = (z ^ key_z) * n_y + (y ^ key_y)
            first = (n_z * n_y - 1 - query_block + key_block) * local_len
            columns.append(pl.ds(pl.multiple_of(first, local_len), local_len))
    return columns


def split_keys(dims, seq_count, heads, size, kv_refs, offset, plain_ref, turned_ref):
    n_z, _, local_len = dims
    for head in range(heads):
        lo, hi = offset + head * size, offset + (head + 1) * size
        for s in range(seq_count):
            index = head * seq_count + s
            for group, kv_ref in enumerate(kv_refs):
                for key_z in range(n_z):
                    at = (key_z * seq_count + s) * local_len
                    to = (group * n_z + key_z) * local_len
                    block = kv_ref[at : at + local_len, lo:hi]
                    if plain_ref is not None:
                        plain_ref[index, to : to + local_len, :] = block
                    if turned_ref is not None:
                        turned_ref[index, :, to : to + local_len] = block.T


def attn_fwd_kernel(dims, seq_count, heads, size, key_ys, first, pos_ref, vec_ref, q_ref, *refs):
    n_z, _, local_len = dims
    kv_refs, refs = refs[: len(key_ys)], refs[len(key_ys) :]
    if first:
        out_ref, *refs = refs
    else:
        out_in, c_ref, out_ref, *refs = refs
    tile_ref, kt_ref, v_ref, qh_ref = refs
    inner = heads * size
    split_keys(dims, seq_count, heads, size, kv_refs, 0, None, kt_ref)
    split_keys(dims, seq_count, heads, size, kv_refs, inner, v_ref, None)
    for head in range(heads):
        qh_ref[head] = q_ref[:, head * size : (head + 1) * size]

    def head_step(head, carry):
        bias_tile(vec_ref, tile_ref, head)

        def query_step(query_z, carry):
            columns = key_columns(pos_ref, dims, key_ys, query_z)
            for s in range(seq_count):
                row = pl.multiple_of((query_z * seq_count + s) * local_len, local_len)
                rows = pl.ds(row, local_len)
                bias = jnp.concatenate([tile_ref[:, c] for c in columns], axis=1)
                score = dot_nn(qh_ref[head, rows, :], kt_ref[head * seq_count + s]) + bias
                top = jnp.max(score, axis=1, keepdims=True)
                if not first:
                    top_before = out_in[head, rows, size : size + 1]
                    top = jnp.maximum(top, top_before)
                weight = jnp.exp(score - top)
                total = jnp.sum(weight, axis=1, keepdims=True)
                out = dot_nn(weight.astype(bf16), v_ref[head * seq_count + s])
                if first:
                    out_ref[head, rows, :size] = out
                    out_ref[head, rows, size : size + 1] = top
                    out_ref[head, rows, size + 1 : size + 2] = total
                else:
                    fade = jnp.exp(top_before - top)
                    total = total + fade * out_in[head, rows, size + 1 : size + 2]
                    out_ref[head, rows, :size] = (out + fade * out_in[head, rows, :size]) / total
                    out_ref[head, rows, size : size + 1] = top + jnp.log(total)
            return carry

        return lax.fori_loop(0, n_z, query_step, carry, unroll=2)

    lax.fori_loop(0, heads, head_step, 0)
    if not first:
        for head in range(heads):
            c_ref[:, head * size : (head + 1) * size] = out_ref[head, :, :size].astype(bf16)


def attn_bwd_kernel(dims, seq_count, heads, size, key_ys, first, pos_ref, vec_ref, q_ref, *refs):
    n_z, _, local_len = dims
    count = len(key_ys)
    dc_ref, c_ref, *refs = refs
    kv_refs, refs = refs[:count], refs[count:]
    if first:
        dq_ref, diag_ref, *refs = refs
        dqh_ref = dq_ref
    else:
        dq_in, diag_in, dq_ref, diag_ref, *refs = refs
    dkv_refs, refs = refs[:count], refs[count:]
    tile_ref, grad_ref, kt_ref, vt_ref, k_ref, qh_ref, dch_ref, delta_ref, dk_ref, dv_ref = refs[:10]
    if not first:
        dqh_ref = refs[10]
    inner = heads * size
    split_keys(dims, seq_count, heads, size, kv_refs, 0, k_ref, kt_ref)
    split_keys(dims, seq_count, heads, size, kv_refs, inner, None, vt_ref)
    for head in range(heads):
        qh_ref[head] = q_ref[:, head * size : (head + 1) * size]
        dc = dc_ref[:, head * size : (head + 1) * size]
        dch_ref[head] = dc
        delta_ref[head] = jnp.sum(dc.astype(f32) * c_ref[head, :, :size], axis=1, keepdims=True)
    if first:
        diag_ref[...] = jnp.zeros_like(diag_ref)
    else:
        diag_ref[...] = diag_in[...]
    dk_ref[...] = jnp.zeros_like(dk_ref)
    dv_ref[...] = jnp.zeros_like(dv_ref)

    def head_step(head, carry):
        bias_tile(vec_ref, tile_ref, head)
        grad_ref[...] = jnp.zeros_like(grad_ref)

        def query_step(query_z, carry):
            columns = key_columns(pos_ref, dims, key_ys, query_z)
            for s in range(seq_count):
                index = head * seq_count + s
                row = pl.multiple_of((query_z * seq_count + s) * local_len, local_len)
                rows = pl.ds(row, local_len)
                q = qh_ref[head, rows, :]
                dc = dch_ref[head, rows, :]
                bias = jnp.concatenate([tile_ref[:, c] for c in columns], axis=1)
                prob = jnp.exp(dot_nn(q, kt_ref[index]) + bias - c_ref[head, rows, size : size + 1])
                dprob = dot_nn(dc, vt_ref[index])
                ds_f = prob * (dprob - delta_ref[head, rows, :])
                ds = ds_f.astype(bf16)
                dq = dot_nn(ds, k_ref[index])
                if not first:
                    dq = dq + dq_in[head, rows, :]
                dqh_ref[head, rows, :] = dq
                dk_ref[index] += dot_tn(q, ds)
                dv_ref[index] += dot_tn(dc, prob.astype(bf16))
                for i, c in enumerate(columns):
                    grad_ref[:, c] += ds_f[:, i * local_len : (i + 1) * local_len]
            return carry

        lax.fori_loop(0, n_z, query_step, 0, unroll=2)
        folded = grad_ref[...]
        width = folded.shape[1]
        while folded.shape[0] > 1:
            half = folded.shape[0] // 2
            folded = folded[:half] + pltpu.roll(folded[half:], width - half, 1)
        diag_ref[pl.ds(head, 1), :] += folded
        return carry

    lax.fori_loop(0, heads, head_step, 0)
    for head in range(heads):
        lo, hi = head * size, (head + 1) * size
        if not first:
            dq_ref[:, lo:hi] = dqh_ref[head].astype(bf16)
        for s in range(seq_count):
            index = head * seq_count + s
            for group, out in enumerate(dkv_refs):
                for key_z in range(n_z):
                    at = (key_z * seq_count + s) * local_len
                    to = (group * n_z + key_z) * local_len
                    cut = slice(to, to + local_len)
                    out[at : at + local_len, lo:hi] = dk_ref[index, :, cut].T.astype(out.dtype)
                    out[at : at + local_len, inner + lo : inner + hi] = dv_ref[
                        index, :, cut
                    ].T.astype(out.dtype)


def vmem_specs(count):
    return [pl.BlockSpec(memory_space=pltpu.VMEM) for _ in range(count)]


def attn_fwd(dims, seq_count, heads, size, key_ys, pos, vec, q, kvs, before=()):
    rows = q.shape[0]
    length = len(key_ys) * dims[0] * dims[2]
    both = heads * seq_count
    first = not before
    wide = jax.ShapeDtypeStruct((heads, rows, 2 * size), f32)
    joined = jax.ShapeDtypeStruct((rows, heads * size), bf16)
    return pl.pallas_call(
        partial(attn_fwd_kernel, dims, seq_count, heads, size, key_ys, first),
        out_shape=(wide,) if first else (joined, wide),
        in_specs=[pl.BlockSpec(memory_space=pltpu.SMEM)]
        + vmem_specs(2 + len(kvs) + len(before)),
        out_specs=tuple(vmem_specs(1 if first else 2)),
        scratch_shapes=[
            pltpu.VMEM((dims[2], vec.shape[1]), f32),
            pltpu.VMEM((both, size, length), bf16),
            pltpu.VMEM((both, length, size), bf16),
            pltpu.VMEM((heads, rows, size), bf16),
        ],
        compiler_params=pltpu.CompilerParams(vmem_limit_bytes=VMEM),
        cost_estimate=effort(5000 * heads * rows * length),
        name="attn_fwd",
    )(pos, vec, q, *kvs, *before)


def attn_bwd(dims, seq_count, heads, size, key_ys, pos, vec, q, dc, c, kvs, before=()):
    rows = q.shape[0]
    length = len(key_ys) * dims[0] * dims[2]
    both = heads * seq_count
    first = not before
    wide = jax.ShapeDtypeStruct((heads, rows, size), f32)
    joined = jax.ShapeDtypeStruct((rows, heads * size), bf16)
    shapes = [wide if first else joined, jax.ShapeDtypeStruct(vec.shape, f32)]
    for key_y in key_ys:
        shapes.append(jax.ShapeDtypeStruct(kvs[0].shape, bf16 if key_y else f32))
    scratch = [
        pltpu.VMEM((dims[2], vec.shape[1]), f32),
        pltpu.VMEM((dims[2], vec.shape[1]), f32),
        pltpu.VMEM((both, size, length), bf16),
        pltpu.VMEM((both, size, length), bf16),
        pltpu.VMEM((both, length, size), bf16),
        pltpu.VMEM((heads, rows, size), bf16),
        pltpu.VMEM((heads, rows, size), bf16),
        pltpu.VMEM((heads, rows, 1), f32),
        pltpu.VMEM((both, size, length), f32),
        pltpu.VMEM((both, size, length), f32),
    ]
    if not first:
        scratch.append(pltpu.VMEM((heads, rows, size), f32))
    return pl.pallas_call(
        partial(attn_bwd_kernel, dims, seq_count, heads, size, key_ys, first),
        out_shape=tuple(shapes),
        in_specs=[pl.BlockSpec(memory_space=pltpu.SMEM)]
        + vmem_specs(4 + len(kvs) + len(before)),
        out_specs=tuple(vmem_specs(len(shapes))),
        scratch_shapes=scratch,
        compiler_params=pltpu.CompilerParams(vmem_limit_bytes=VMEM),
        cost_estimate=effort(7500 * heads * rows * length),
        name="attn_bwd",
    )(pos, vec, q, dc, c, *kvs, *before)


def gelu_parts(pre):
    square = pre * pre
    tanh = jnp.tanh(0.7978845608028654 * (pre + 0.044715 * pre * square))
    hidden = 0.5 * pre * (1.0 + tanh)
    slope = 0.5 * (1.0 + tanh) + 0.5 * pre * (1.0 - tanh * tanh) * (
        0.7978845608028654 * (1.0 + 0.134145 * square)
    )
    return hidden.astype(bf16), slope


def accumulate(out_ref, acc_ref, value):
    step = pl.program_id(0)

    @pl.when(step == 0)
    def _():
        acc_ref[...] = value

    @pl.when(step > 0)
    def _():
        acc_ref[...] += value

    @pl.when(step == pl.num_programs(0) - 1)
    def _():
        out_ref[...] = acc_ref[...].astype(out_ref.dtype)


def expert_own_kernel(rows_ref, dy_ref, weight_ref, y_ref, db_ref, g_ref, du_ref, y_acc, db_acc):
    hidden, slope = gelu_parts(dot_nn(rows_ref[...], weight_ref[0, 0]))
    g_ref[0] = hidden
    accumulate(y_ref, y_acc, dot_nt(hidden, weight_ref[0, 1]))
    du = (dot_nn(dy_ref[...], weight_ref[0, 1]) * slope).astype(bf16)
    du_ref[0] = du
    accumulate(db_ref, db_acc, dot_nt(du, weight_ref[0, 0]))


def expert_fwd_kernel(rows_ref, weight_ref, y_ref, g_ref, slope_ref, y_acc):
    hidden, slope = gelu_parts(dot_nn(rows_ref[...], weight_ref[0, 0]))
    g_ref[0] = hidden
    slope_ref[0] = slope.astype(bf16)
    accumulate(y_ref, y_acc, dot_nt(hidden, weight_ref[0, 1]))


def expert_bwd_kernel(dy_ref, slope_ref, weight_ref, db_ref, du_ref, db_acc):
    du = (dot_nn(dy_ref[...], weight_ref[0, 1]) * slope_ref[0].astype(f32)).astype(bf16)
    du_ref[0] = du
    accumulate(db_ref, db_acc, dot_nt(du, weight_ref[0, 0]))


def expert_call(kernel, name, rows, kept_in, up_down, out_type, wholes):
    count = rows[0].shape[0]
    n_z, _, width, hidden = up_down.shape
    whole = pl.BlockSpec((count, width), lambda i: (0, 0))
    weight = pl.BlockSpec((1, 2, width, hidden), lambda i: (i, 0, 0, 0))
    kept = pl.BlockSpec((1, count, hidden), lambda i: (i, 0, 0))
    kept_out = 1 if kept_in else 2
    return pl.pallas_call(
        kernel,
        grid=(n_z,),
        out_shape=(jax.ShapeDtypeStruct((count, width), out_type),) * wholes
        + (jax.ShapeDtypeStruct((n_z, count, hidden), bf16),) * kept_out,
        in_specs=[whole] * len(rows) + [kept] * len(kept_in) + [weight],
        out_specs=(whole,) * wholes + (kept,) * kept_out,
        scratch_shapes=[pltpu.VMEM((count, width), f32)] * wholes,
        compiler_params=pltpu.CompilerParams(vmem_limit_bytes=VMEM),
        cost_estimate=effort(12 * count * width * hidden * n_z * wholes),
        name=name,
    )(*rows, *kept_in, up_down)


def expert_grad_kernel(b_ref, b_other, dy_ref, dy_other, du_ref, du_other, g_ref, g_other, out_ref):
    grad_up = dot_tn(b_ref[...], du_ref[0]) + dot_tn(b_other[...], du_other[0])
    out_ref[0, 0] = grad_up.astype(bf16)
    grad_down = dot_tn(dy_ref[...], g_ref[0]) + dot_tn(dy_other[...], g_other[0])
    out_ref[0, 1] = grad_down.astype(bf16)


def expert_grad(rows, kept):
    width = rows[2].shape[1]
    n_z, _, hidden = kept[0].shape
    return pl.pallas_call(
        expert_grad_kernel,
        grid=(n_z,),
        out_shape=jax.ShapeDtypeStruct((n_z, 2, width, hidden), bf16),
        in_specs=[pl.BlockSpec((v.shape[0], width), lambda i: (0, 0)) for v in rows]
        + [pl.BlockSpec((1,) + v.shape[1:], lambda i: (i, 0, 0)) for v in kept],
        out_specs=pl.BlockSpec((1, 2, width, hidden), lambda i: (i, 0, 0, 0)),
        compiler_params=pltpu.CompilerParams(vmem_limit_bytes=VMEM),
        cost_estimate=effort(5 * 2 * sum(v.shape[0] for v in rows) * width * hidden * n_z),
        name="expert_grad",
    )(*rows, *kept)


def weight_grad_kernel(a_ref, grad_ref, out_grad_ref, context_ref, small_ref, out_ref):
    cut = grad_ref.shape[1]
    wide = cut + small_ref.shape[1]
    out_ref[:, :cut] = dot_tn(a_ref[...], grad_ref[...]).astype(bf16)
    out_ref[:, cut:wide] = small_ref[...].astype(bf16)
    out_ref[:, wide:] = dot_tn(out_grad_ref[...], context_ref[...]).astype(bf16)


def weight_grad(a, grad, out_grad, context, small):
    width = a.shape[1]
    columns = grad.shape[1] + small.shape[1] + context.shape[1]
    return pl.pallas_call(
        weight_grad_kernel,
        out_shape=jax.ShapeDtypeStruct((width, columns), bf16),
        in_specs=vmem_specs(5),
        out_specs=vmem_specs(1)[0],
        compiler_params=pltpu.CompilerParams(vmem_limit_bytes=VMEM),
        cost_estimate=effort(4 * 2 * a.shape[0] * width * columns),
        name="weight_grad",
    )(a, grad, out_grad, context, small)


def local(
    tokens,
    cotangent,
    gain_attn,
    query_w,
    key_w,
    value_w,
    output_w,
    rel_table,
    rel_bucket,
    gain_ffn,
    router_w,
    routes,
    expert_in,
    expert_out,
):
    seq_count, local_len, width = tokens.shape
    tok = seq_count * local_len
    n_dp, n_seq = lax.axis_size("dp"), lax.axis_size("seq")
    head_count = rel_table.shape[1]
    inner = query_w.shape[1]
    size = inner // head_count
    n_z = math.gcd(head_count, n_seq)
    n_y = n_seq // n_z
    heads = head_count // n_z
    part = heads * size
    experts = router_w.shape[1]
    capacity = 2 * tok // experts
    table_rows = rel_table.shape[0]
    buckets = table_rows * n_seq
    w_rows = query_w.shape[0]
    dims = (n_z, n_y, local_len)
    dp, seq = lax.axis_index("dp"), lax.axis_index("seq")
    z, y = seq // n_y, seq % n_y
    dp_bits, y_bits, z_bits = bits_of(n_dp), bits_of(n_y), bits_of(n_z)

    def swap_z(value, k):
        return swap(value, "seq", k * n_y) if k else value

    def swap_y(value, k):
        return swap(value, "seq", k) if k else value

    def swap_dp(value, k):
        return swap(value, "dp", k) if k else value

    extra = jnp.concatenate([gain_attn[:, None], gain_ffn[:, None], router_w], axis=1)
    extra = jnp.broadcast_to(extra[None], (n_z, w_rows, 2 + experts))
    table_at = part * 3 + 2 + experts
    table = rel_table.reshape(table_rows, n_z, heads).transpose(1, 0, 2)
    table = jnp.pad(table, ((0, 0), (0, w_rows - table_rows), (0, 0)))
    joined = [w.reshape(w_rows, n_z, part).transpose(1, 0, 2) for w in (query_w, key_w, value_w)]
    pack = jnp.concatenate(joined + [extra, table], axis=2)
    packed = -(-pack.shape[2] // 128) * 128
    pack = jnp.pad(pack, ((0, 0), (0, 0), (0, packed - pack.shape[2])))
    by_partner = unxor([pack[j] for j in range(n_z)], z)
    out_t = output_w.T
    by_partner = [jnp.concatenate([v, out_t], axis=1) for v in by_partner]
    gathered = jnp.stack(unxor([swap_z(by_partner[k], k) for k in range(n_z)], z))

    x_own = tokens.reshape(tok, width)
    upward = [(i, i + n_y) for i in range(n_seq - n_y)]
    downward = [(i + n_y, i) for i in range(n_seq - n_y)]
    below, above = [x_own], [x_own]
    for _ in range(n_z - 1):
        below.append(lax.ppermute(below[-1], "seq", upward))
        above.append(lax.ppermute(above[-1], "seq", downward))
    x_parts = [x_own]
    for k in range(1, n_z):
        chosen = x_own
        for j in range(n_z):
            source = j ^ k
            value = below[j - source] if source < j else above[source - j]
            chosen = jnp.where(z == j, value, chosen)
        x_parts.append(chosen)

    for bit in y_bits:
        gathered = grow(gathered, "seq", bit, (y & bit) != 0)
    route_ids = routes.reshape(tok)
    choose = route_ids[:, None] == jnp.arange(experts, dtype=jnp.int32)[None, :]
    choose_f = choose.astype(f32)
    before = jnp.arange(tok)[:, None] > jnp.arange(tok)[None, :]
    earlier = dot_nn(before.astype(bf16), choose.astype(bf16))
    slot = jnp.sum(earlier * choose_f, axis=1).astype(jnp.int32)
    place = (route_ids ^ dp) * capacity + slot
    place_hot = jnp.arange(experts * capacity, dtype=jnp.int32)[:, None] == place[None, :]
    place_b = place_hot.astype(bf16)

    def to_experts(values):
        sent = dot_nn(place_b, values).astype(bf16).reshape(experts, capacity, -1)
        return [swap_dp(sent[k], k) for k in range(n_dp)]

    def weigh(values, rows):
        gates = rows[:, width : width + 1].astype(f32) + rows[:, width + 1 : width + 2].astype(f32)
        return (values.astype(f32) * gates).astype(bf16)

    def to_others(parts, *others):
        moved = [swap_y(v, k) for k in range(1, n_y) for v in parts]
        return jnp.concatenate([after(v, *others) for v in moved], axis=0)

    def from_experts(total, *others):
        blocks = total.astype(bf16).reshape(n_dp, capacity, width)
        back = [swap_dp(blocks[k], k) for k in range(n_dp)]
        if others:
            back = [after(v, *others) for v in back]
        return dot_tn(place_b, jnp.concatenate(back, axis=0))

    def swap_others(values):
        split = values.reshape(n_y - 1, n_dp * capacity, width)
        return [swap_y(split[k - 1], k) for k in range(1, n_y)]

    upstream_b = cotangent.reshape(tok, width)
    upstream = upstream_b.astype(f32)

    for bit in reversed(dp_bits):
        gathered = grow(gathered, "dp", bit, (dp & bit) != 0)
    n_bits, m_bits = len(y_bits), len(dp_bits)
    order = tuple(reversed(range(m_bits))) + (m_bits + n_bits,)
    order = order + tuple(range(m_bits, m_bits + n_bits)) + (m_bits + n_bits + 1, m_bits + n_bits + 2)
    gathered = gathered.transpose(order).reshape(width, packed + inner)
    out_t = gathered[:, packed:]
    w_qkv = gathered[:, : 3 * part]
    gain_a = gathered[:, 3 * part].astype(f32)
    gain_f = gathered[:, 3 * part + 1].astype(f32)
    w_router = gathered[:, 3 * part + 2 : 3 * part + 2 + experts]
    table = gathered.reshape(n_dp, n_seq, w_rows, packed + inner)[0, :, :table_rows, table_at : table_at + heads]
    table = table.reshape(buckets, heads)

    z_groups = [[j * n_y + i for j in range(n_z)] for i in range(n_y)]
    up_down = jnp.stack([expert_in[0], expert_out[0]])
    x_all, up_down = lax.optimization_barrier((jnp.concatenate(x_parts, axis=0), up_down))
    up_down = lax.all_gather(up_down, "seq", axis=0, axis_index_groups=z_groups)

    x_all = x_all.astype(f32)
    scale_all = lax.rsqrt(jnp.mean(x_all * x_all, axis=-1, keepdims=True) + epsilon)
    normed_all = (x_all * scale_all * gain_a).astype(bf16)
    kv = dot_nn(normed_all, w_qkv[:, part:]).astype(bf16)
    kvs = [swap_y(kv, k) for k in range(n_y)]
    q = dot_nn(normed_all, w_qkv[:, :part]).astype(bf16)
    d_rows = to_experts(after(upstream_b, x_all))
    span = 2 * n_seq * local_len
    bucket_pad = jnp.concatenate([rel_bucket, jnp.full((1,), -1, jnp.int32)])
    bucket_hot = bucket_pad[None, :] == jnp.arange(buckets, dtype=jnp.int32)[:, None]
    table_pad = jnp.pad(table, ((0, 0), (0, 8 - heads)))
    vec = dot_tn(table_pad, bucket_hot.astype(bf16))
    pos = jnp.stack([z, y]).astype(jnp.int32)
    others = tuple(range(1, n_y))
    shape = (dims, seq_count, heads, size)
    before = attn_fwd(*shape, (0,), pos, vec, q, kvs[:1])
    d_rows = [after(v, *before) for v in d_rows]
    d_own = jnp.concatenate(d_rows, axis=0)
    context_parts, context_f = attn_fwd(*shape, others, pos, vec, q, kvs[1:], before)
    d_other = to_others(d_rows, context_parts)
    context_parts = after(context_parts, *d_rows).reshape(n_z, tok, part)
    context = [swap_z(context_parts[k], k) for k in range(n_z)]
    context = jnp.concatenate(unxor(context, z), axis=1)

    inputs = x_own.astype(f32)
    hidden_attn = inputs + dot_nt(context, out_t)
    scale_f = lax.rsqrt(jnp.mean(hidden_attn * hidden_attn, axis=-1, keepdims=True) + epsilon)
    normed_f = (hidden_attn * scale_f * gain_f).astype(bf16)
    logits = dot_nn(normed_f, w_router)
    router_p = jax.nn.softmax(logits, axis=-1)
    gate = jnp.sum(router_p * choose_f, axis=-1)

    gate_high = gate.astype(bf16)
    gate_low = (gate - gate_high.astype(f32)).astype(bf16)
    b_gate = jnp.stack([gate_high, gate_low], axis=1)
    b_gate = jnp.pad(b_gate, ((0, 0), (0, 126)))
    b_rows = to_experts(jnp.concatenate([normed_f, b_gate], axis=1))
    b_own = jnp.concatenate(b_rows, axis=0)
    dy_own = weigh(d_own, b_own)
    b_other = to_others(b_rows)
    dy_other = weigh(d_other, b_other)
    y_other, g_other, slope = expert_call(
        expert_fwd_kernel, "expert_fwd", (b_other,), (), up_down, bf16, 1
    )
    db_other, du_other = expert_call(
        expert_bwd_kernel, "expert_bwd", (dy_other,), (slope,), up_down, bf16, 1
    )
    y_got = swap_others(y_other)
    db_got = swap_others(db_other)
    b_own = after(b_own, db_other, *y_got)
    y_own, db_own, g_own, du_own = expert_call(
        expert_own_kernel, "expert_own", (b_own, dy_own), (), up_down, f32, 2
    )
    y_total = y_own + sum(v.astype(f32) for v in y_got)
    db_total = db_own + sum(v.astype(f32) for v in db_got)
    expert_tok = from_experts(y_total)
    grad_up_down = expert_grad(
        (b_own, b_other, after(dy_own, db_total), dy_other), (du_own, du_other, g_own, g_other)
    )
    grad_normed = from_experts(db_total, grad_up_down)
    grad_up_down = lax.psum_scatter(
        grad_up_down, "seq", scatter_dimension=0, axis_index_groups=z_groups, tiled=True
    )
    grad_up = grad_up_down[:, 0].astype(f32)
    grad_down = grad_up_down[:, 1].astype(f32)

    mixed = (hidden_attn + gate[:, None] * expert_tok).astype(bf16).reshape(tokens.shape)
    grad_gate = jnp.sum(upstream * expert_tok, axis=-1)
    grad_logits = grad_gate[:, None] * router_p * (choose_f - gate[:, None])
    grad_router = lax.dot_general(
        normed_f.astype(f32), grad_logits, (((0,), (0,)), ((), ())), precision=highest
    )
    grad_normed = grad_normed + lax.dot_general(
        grad_logits, w_router.astype(f32), (((1,), (1,)), ((), ())), precision=highest
    )
    scaled = gain_f * grad_normed
    grad_hidden = upstream + scale_f * scaled
    grad_hidden = grad_hidden - hidden_attn * scale_f**3 * jnp.mean(
        scaled * hidden_attn, axis=-1, keepdims=True
    )
    grad_gain_f = jnp.sum(grad_normed * hidden_attn * scale_f, axis=0)
    grad_attn = grad_hidden.astype(bf16)

    grad_ctx = dot_nn(grad_attn, out_t).astype(bf16)
    grad_ctx = unxor([grad_ctx[:, j * part : (j + 1) * part] for j in range(n_z)], z)
    grad_ctx = jnp.concatenate([swap_z(grad_ctx[k], k) for k in range(n_z)], axis=0)
    grad_q, diag, *grad_kvs = attn_bwd(
        *shape, others, pos, vec, q, grad_ctx, context_f, kvs[1:]
    )
    arrived = [swap_y(grad_kvs[k - 1], k) for k in range(1, n_y)]
    grad_q, diag, grad_kv = attn_bwd(
        *shape, (0,), pos, vec, q, grad_ctx, context_f, kvs[:1], (grad_q, diag)
    )
    for value in arrived:
        grad_kv = grad_kv + value.astype(f32)
    grad_qkv = jnp.concatenate([grad_q, grad_kv.astype(bf16)], axis=1)
    odd, even = list(range(1, n_z, 2)), list(range(0, n_z, 2))

    def take(value, blocks):
        value = value.reshape(n_z, tok, value.shape[1])
        return jnp.concatenate([value[k] for k in blocks], axis=0)

    sent = dot_nt(take(grad_qkv, odd), w_qkv)
    got = swap_z(sent.astype(bf16), 1)
    kept = dot_nt(take(grad_qkv, even), w_qkv)
    grad_gain_a = jnp.sum(sent * take(x_all * scale_all, odd), axis=0)
    grad_gain_a = grad_gain_a + jnp.sum(kept * take(x_all * scale_all, even), axis=0)
    diag = jnp.roll(diag, local_len - 1, axis=1)
    grad_table = lax.dot_general(
        diag, bucket_hot.astype(f32), (((1,), (1,)), ((), ())), precision=highest
    )
    grad_table = grad_table[:heads].T.reshape(1, n_seq, table_rows, heads)
    grad_table = jnp.pad(grad_table, ((0, 0), (0, 0), (0, w_rows - table_rows), (0, 0)))
    grad_table = jnp.broadcast_to(grad_table, (n_dp, n_seq, w_rows, heads)).reshape(width, heads)
    small = [grad_gain_a[:, None], grad_gain_f[:, None], grad_router, grad_table]
    small = jnp.concatenate(small, axis=1)
    small = jnp.pad(small, ((0, 0), (0, packed - 3 * part - small.shape[1])))
    value = weight_grad(normed_all, grad_qkv, grad_attn, context, small)
    value = value.reshape((2,) * m_bits + (n_z,) + (2,) * n_bits + (w_rows, packed + inner))
    for i, bit in enumerate(dp_bits):
        value = halve(value, m_bits - 1 - i, "dp", bit, (dp & bit) != 0)
    got = after(got, value)
    grad_a = (kept + got.astype(f32)).reshape(n_z // 2, tok, width)
    for bit in bits_of(n_z // 2):
        half = [k for k in range(0, grad_a.shape[0], 2)]
        far = jnp.concatenate([grad_a[k + 1] for k in half]).astype(bf16)
        far = swap_z(far, 2 * bit)
        grad_a = jnp.stack([grad_a[k] for k in half])
        if len(half) > 1:
            grad_a = grad_a + far.astype(f32).reshape(len(half), tok, width)
    for i, bit in enumerate(y_bits):
        value = halve(value, n_bits - i, "seq", bit, (y & bit) != 0)
    value = after(value, grad_a, grad_up_down)
    parts = unxor([value[j] for j in range(n_z)], z)
    summed = unxor([swap_z(parts[k], k) for k in range(n_z)], z)
    grad_query, grad_key, grad_value = (
        jnp.concatenate([v[:, i * part : (i + 1) * part] for v in summed], axis=1).astype(f32)
        for i in range(3)
    )
    total = sum(v[:, 3 * part :].astype(f32) for v in summed)
    grad_gain_attn = total[:, 0]
    grad_gain_ffn = total[:, 1]
    grad_router = total[:, 2 : 2 + experts]
    grad_output = total[:, packed - 3 * part :].T
    grad_table = jnp.concatenate(
        [v[:table_rows, table_at : table_at + heads] for v in summed], axis=1
    ).astype(f32)

    far, grad_output = lax.optimization_barrier((far, grad_output))
    grad_a = grad_a[0] + far.astype(f32)
    scale_a = scale_all[:tok]
    scaled_a = gain_a * grad_a
    grad_x = grad_hidden + scale_a * scaled_a
    grad_x = grad_x - inputs * scale_a**3 * jnp.mean(scaled_a * inputs, axis=-1, keepdims=True)
    grad_tokens = grad_x.reshape(tokens.shape)

    return (
        mixed,
        grad_tokens,
        grad_gain_attn,
        grad_query,
        grad_key,
        grad_value,
        grad_output,
        grad_table,
        grad_gain_ffn,
        grad_router,
        grad_up,
        grad_down,
    )


def solution(mesh):
    vector = P(("dp", "seq"))
    matrix = P(("dp", "seq"), None)
    rows = P("dp", "seq", None)
    expert = P("dp", None, "seq")
    last = P(None, ("dp", "seq"))
    table = P("seq", None)
    return jax.shard_map(
        local,
        mesh=mesh,
        in_specs=(
            rows,
            rows,
            vector,
            matrix,
            matrix,
            matrix,
            last,
            table,
            P(),
            vector,
            matrix,
            P("dp", "seq", None, None),
            expert,
            expert,
        ),
        out_specs=(
            rows,
            rows,
            vector,
            matrix,
            matrix,
            matrix,
            last,
            table,
            vector,
            matrix,
            expert,
            expert,
        ),
        check_vma=False,
    )
```

```python
import math
from functools import partial

import jax
import jax.numpy as jnp
from jax import lax
from jax.experimental import pallas as pl
from jax.experimental.pallas import tpu as pltpu
from jax.sharding import PartitionSpec as P

epsilon = 1e-06
highest = lax.Precision.HIGHEST
bf16 = jnp.bfloat16
f32 = jnp.float32
VMEM = 56 * 1024 * 1024


def effort(flops):
    return pl.CostEstimate(flops=int(flops), transcendentals=0, bytes_accessed=int(flops) // 320)


def dot_nn(left, right):
    return lax.dot_general(left, right, (((1,), (0,)), ((), ())), preferred_element_type=f32)


def dot_tn(left, right):
    return lax.dot_general(left, right, (((0,), (0,)), ((), ())), preferred_element_type=f32)


def dot_nt(left, right):
    return lax.dot_general(left, right, (((1,), (1,)), ((), ())), preferred_element_type=f32)


def swap(value, axis, mask):
    size = lax.axis_size(axis)
    return lax.ppermute(value, axis, [(i, i ^ mask) for i in range(size)])


def bits_of(size):
    return [1 << i for i in range(size.bit_length() - 1)]


def unxor(parts, index):
    for bit in bits_of(len(parts)):
        flag = (index & bit) != 0
        parts = [jnp.where(flag, parts[j ^ bit], parts[j]) for j in range(len(parts))]
    return parts


def after(value, *others):
    return lax.optimization_barrier((value, *others))[0]


def grow(value, axis, mask, bit_set):
    other = swap(value, axis, mask)
    return jnp.stack([jnp.where(bit_set, other, value), jnp.where(bit_set, value, other)])


def pick(value, position, flag):
    low = lax.index_in_dim(value, 0, position, keepdims=False)
    high = lax.index_in_dim(value, 1, position, keepdims=False)
    return jnp.where(flag, high, low)


def halve(value, position, axis, mask, bit_set):
    sent = pick(value, position, jnp.logical_not(bit_set))
    kept = pick(value, position, bit_set)
    got = swap(sent, axis, mask)
    return (kept.astype(f32) + got.astype(f32)).astype(bf16)


def bias_tile(vec_ref, tile_ref, head):
    rows, width = tile_ref.shape
    vec = jnp.broadcast_to(vec_ref[pl.ds(head, 1), :], (rows, width))
    tile_ref[...] = pltpu.roll(vec, width - (rows - 1), 1, stride=1, stride_axis=0)


def key_columns(pos_ref, dims, key_ys, query_z):
    n_z, n_y, local_len = dims
    z, y = pos_ref[0], pos_ref[1]
    query_block = (z ^ query_z) * n_y + y
    columns = []
    for key_y in key_ys:
        for key_z in range(n_z):
            key_block = (z ^ key_z) * n_y + (y ^ key_y)
            first = (n_z * n_y - 1 - query_block + key_block) * local_len
            columns.append(pl.ds(pl.multiple_of(first, local_len), local_len))
    return columns


def split_keys(dims, seq_count, heads, size, kv_refs, offset, plain_ref, turned_ref):
    n_z, _, local_len = dims
    for head in range(heads):
        lo, hi = offset + head * size, offset + (head + 1) * size
        for s in range(seq_count):
            index = head * seq_count + s
            for group, kv_ref in enumerate(kv_refs):
                for key_z in range(n_z):
                    at = (key_z * seq_count + s) * local_len
                    to = (group * n_z + key_z) * local_len
                    block = kv_ref[at : at + local_len, lo:hi]
                    if plain_ref is not None:
                        plain_ref[index, to : to + local_len, :] = block
                    if turned_ref is not None:
                        turned_ref[index, :, to : to + local_len] = block.T


def attn_fwd_kernel(dims, seq_count, heads, size, key_ys, first, pos_ref, vec_ref, q_ref, *refs):
    n_z, _, local_len = dims
    kv_refs, refs = refs[: len(key_ys)], refs[len(key_ys) :]
    if first:
        out_ref, *refs = refs
    else:
        out_in, c_ref, out_ref, *refs = refs
    tile_ref, kt_ref, v_ref, qh_ref = refs
    inner = heads * size
    split_keys(dims, seq_count, heads, size, kv_refs, 0, None, kt_ref)
    split_keys(dims, seq_count, heads, size, kv_refs, inner, v_ref, None)
    for head in range(heads):
        qh_ref[head] = q_ref[:, head * size : (head + 1) * size]

    def head_step(head, carry):
        bias_tile(vec_ref, tile_ref, head)

        def query_step(query_z, carry):
            columns = key_columns(pos_ref, dims, key_ys, query_z)
            for s in range(seq_count):
                row = pl.multiple_of((query_z * seq_count + s) * local_len, local_len)
                rows = pl.ds(row, local_len)
                bias = jnp.concatenate([tile_ref[:, c] for c in columns], axis=1)
                score = dot_nn(qh_ref[head, rows, :], kt_ref[head * seq_count + s]) + bias
                top = jnp.max(score, axis=1, keepdims=True)
                if not first:
                    top_before = out_in[head, rows, size : size + 1]
                    top = jnp.maximum(top, top_before)
                weight = jnp.exp(score - top)
                total = jnp.sum(weight, axis=1, keepdims=True)
                out = dot_nn(weight.astype(bf16), v_ref[head * seq_count + s])
                if first:
                    out_ref[head, rows, :size] = out
                    out_ref[head, rows, size : size + 1] = top
                    out_ref[head, rows, size + 1 : size + 2] = total
                else:
                    fade = jnp.exp(top_before - top)
                    total = total + fade * out_in[head, rows, size + 1 : size + 2]
                    out_ref[head, rows, :size] = (out + fade * out_in[head, rows, :size]) / total
                    out_ref[head, rows, size : size + 1] = top + jnp.log(total)
            return carry

        return lax.fori_loop(0, n_z, query_step, carry, unroll=2)

    lax.fori_loop(0, heads, head_step, 0)
    if not first:
        for head in range(heads):
            c_ref[:, head * size : (head + 1) * size] = out_ref[head, :, :size].astype(bf16)


def attn_bwd_kernel(dims, seq_count, heads, size, key_ys, first, pos_ref, vec_ref, q_ref, *refs):
    n_z, _, local_len = dims
    count = len(key_ys)
    dc_ref, c_ref, *refs = refs
    kv_refs, refs = refs[:count], refs[count:]
    if first:
        dq_ref, diag_ref, *refs = refs
        dqh_ref = dq_ref
    else:
        dq_in, diag_in, dq_ref, diag_ref, *refs = refs
    dkv_refs, refs = refs[:count], refs[count:]
    tile_ref, grad_ref, kt_ref, vt_ref, k_ref, qh_ref, dch_ref, delta_ref, dk_ref, dv_ref = refs[:10]
    if not first:
        dqh_ref = refs[10]
    inner = heads * size
    split_keys(dims, seq_count, heads, size, kv_refs, 0, k_ref, kt_ref)
    split_keys(dims, seq_count, heads, size, kv_refs, inner, None, vt_ref)
    for head in range(heads):
        qh_ref[head] = q_ref[:, head * size : (head + 1) * size]
        dc = dc_ref[:, head * size : (head + 1) * size]
        dch_ref[head] = dc
        delta_ref[head] = jnp.sum(dc.astype(f32) * c_ref[head, :, :size], axis=1, keepdims=True)
    if first:
        diag_ref[...] = jnp.zeros_like(diag_ref)
    else:
        diag_ref[...] = diag_in[...]
    dk_ref[...] = jnp.zeros_like(dk_ref)
    dv_ref[...] = jnp.zeros_like(dv_ref)

    def head_step(head, carry):
        bias_tile(vec_ref, tile_ref, head)
        grad_ref[...] = jnp.zeros_like(grad_ref)

        def query_step(query_z, carry):
            columns = key_columns(pos_ref, dims, key_ys, query_z)
            for s in range(seq_count):
                index = head * seq_count + s
                row = pl.multiple_of((query_z * seq_count + s) * local_len, local_len)
                rows = pl.ds(row, local_len)
                q = qh_ref[head, rows, :]
                dc = dch_ref[head, rows, :]
                bias = jnp.concatenate([tile_ref[:, c] for c in columns], axis=1)
                prob = jnp.exp(dot_nn(q, kt_ref[index]) + bias - c_ref[head, rows, size : size + 1])
                dprob = dot_nn(dc, vt_ref[index])
                ds_f = prob * (dprob - delta_ref[head, rows, :])
                ds = ds_f.astype(bf16)
                dq = dot_nn(ds, k_ref[index])
                if not first:
                    dq = dq + dq_in[head, rows, :]
                dqh_ref[head, rows, :] = dq
                dk_ref[index] += dot_tn(q, ds)
                dv_ref[index] += dot_tn(dc, prob.astype(bf16))
                for i, c in enumerate(columns):
                    grad_ref[:, c] += ds_f[:, i * local_len : (i + 1) * local_len]
            return carry

        lax.fori_loop(0, n_z, query_step, 0, unroll=2)
        folded = grad_ref[...]
        width = folded.shape[1]
        while folded.shape[0] > 1:
            half = folded.shape[0] // 2
            folded = folded[:half] + pltpu.roll(folded[half:], width - half, 1)
        diag_ref[pl.ds(head, 1), :] += folded
        return carry

    lax.fori_loop(0, heads, head_step, 0)
    for head in range(heads):
        lo, hi = head * size, (head + 1) * size
        if not first:
            dq_ref[:, lo:hi] = dqh_ref[head].astype(bf16)
        for s in range(seq_count):
            index = head * seq_count + s
            for group, out in enumerate(dkv_refs):
                for key_z in range(n_z):
                    at = (key_z * seq_count + s) * local_len
                    to = (group * n_z + key_z) * local_len
                    cut = slice(to, to + local_len)
                    out[at : at + local_len, lo:hi] = dk_ref[index, :, cut].T.astype(out.dtype)
                    out[at : at + local_len, inner + lo : inner + hi] = dv_ref[
                        index, :, cut
                    ].T.astype(out.dtype)


def vmem_specs(count):
    return [pl.BlockSpec(memory_space=pltpu.VMEM) for _ in range(count)]


def attn_fwd(dims, seq_count, heads, size, key_ys, pos, vec, q, kvs, before=()):
    rows = q.shape[0]
    length = len(key_ys) * dims[0] * dims[2]
    both = heads * seq_count
    first = not before
    wide = jax.ShapeDtypeStruct((heads, rows, 2 * size), f32)
    joined = jax.ShapeDtypeStruct((rows, heads * size), bf16)
    return pl.pallas_call(
        partial(attn_fwd_kernel, dims, seq_count, heads, size, key_ys, first),
        out_shape=(wide,) if first else (joined, wide),
        in_specs=[pl.BlockSpec(memory_space=pltpu.SMEM)]
        + vmem_specs(2 + len(kvs) + len(before)),
        out_specs=tuple(vmem_specs(1 if first else 2)),
        scratch_shapes=[
            pltpu.VMEM((dims[2], vec.shape[1]), f32),
            pltpu.VMEM((both, size, length), bf16),
            pltpu.VMEM((both, length, size), bf16),
            pltpu.VMEM((heads, rows, size), bf16),
        ],
        compiler_params=pltpu.CompilerParams(vmem_limit_bytes=VMEM),
        cost_estimate=effort(5000 * heads * rows * length),
        name="attn_fwd",
    )(pos, vec, q, *kvs, *before)


def attn_bwd(dims, seq_count, heads, size, key_ys, pos, vec, q, dc, c, kvs, before=()):
    rows = q.shape[0]
    length = len(key_ys) * dims[0] * dims[2]
    both = heads * seq_count
    first = not before
    wide = jax.ShapeDtypeStruct((heads, rows, size), f32)
    joined = jax.ShapeDtypeStruct((rows, heads * size), bf16)
    shapes = [wide if first else joined, jax.ShapeDtypeStruct(vec.shape, f32)]
    for key_y in key_ys:
        shapes.append(jax.ShapeDtypeStruct(kvs[0].shape, bf16 if key_y else f32))
    scratch = [
        pltpu.VMEM((dims[2], vec.shape[1]), f32),
        pltpu.VMEM((dims[2], vec.shape[1]), f32),
        pltpu.VMEM((both, size, length), bf16),
        pltpu.VMEM((both, size, length), bf16),
        pltpu.VMEM((both, length, size), bf16),
        pltpu.VMEM((heads, rows, size), bf16),
        pltpu.VMEM((heads, rows, size), bf16),
        pltpu.VMEM((heads, rows, 1), f32),
        pltpu.VMEM((both, size, length), f32),
        pltpu.VMEM((both, size, length), f32),
    ]
    if not first:
        scratch.append(pltpu.VMEM((heads, rows, size), f32))
    return pl.pallas_call(
        partial(attn_bwd_kernel, dims, seq_count, heads, size, key_ys, first),
        out_shape=tuple(shapes),
        in_specs=[pl.BlockSpec(memory_space=pltpu.SMEM)]
        + vmem_specs(4 + len(kvs) + len(before)),
        out_specs=tuple(vmem_specs(len(shapes))),
        scratch_shapes=scratch,
        compiler_params=pltpu.CompilerParams(vmem_limit_bytes=VMEM),
        cost_estimate=effort(7500 * heads * rows * length),
        name="attn_bwd",
    )(pos, vec, q, dc, c, *kvs, *before)


def gelu_parts(pre):
    square = pre * pre
    tanh = jnp.tanh(0.7978845608028654 * (pre + 0.044715 * pre * square))
    hidden = 0.5 * pre * (1.0 + tanh)
    slope = 0.5 * (1.0 + tanh) + 0.5 * pre * (1.0 - tanh * tanh) * (
        0.7978845608028654 * (1.0 + 0.134145 * square)
    )
    return hidden.astype(bf16), slope


def accumulate(out_ref, acc_ref, value):
    step = pl.program_id(0)

    @pl.when(step == 0)
    def _():
        acc_ref[...] = value

    @pl.when(step > 0)
    def _():
        acc_ref[...] += value

    @pl.when(step == pl.num_programs(0) - 1)
    def _():
        out_ref[...] = acc_ref[...].astype(out_ref.dtype)


def expert_own_kernel(rows_ref, dy_ref, weight_ref, y_ref, db_ref, g_ref, du_ref, y_acc, db_acc):
    hidden, slope = gelu_parts(dot_nn(rows_ref[...], weight_ref[0, 0]))
    g_ref[0] = hidden
    accumulate(y_ref, y_acc, dot_nt(hidden, weight_ref[0, 1]))
    du = (dot_nn(dy_ref[...], weight_ref[0, 1]) * slope).astype(bf16)
    du_ref[0] = du
    accumulate(db_ref, db_acc, dot_nt(du, weight_ref[0, 0]))


def expert_fwd_kernel(rows_ref, weight_ref, y_ref, g_ref, slope_ref, y_acc):
    hidden, slope = gelu_parts(dot_nn(rows_ref[...], weight_ref[0, 0]))
    g_ref[0] = hidden
    slope_ref[0] = slope.astype(bf16)
    accumulate(y_ref, y_acc, dot_nt(hidden, weight_ref[0, 1]))


def expert_bwd_kernel(dy_ref, slope_ref, weight_ref, db_ref, du_ref, db_acc):
    du = (dot_nn(dy_ref[...], weight_ref[0, 1]) * slope_ref[0].astype(f32)).astype(bf16)
    du_ref[0] = du
    accumulate(db_ref, db_acc, dot_nt(du, weight_ref[0, 0]))


def expert_call(kernel, name, rows, kept_in, up_down, out_type, wholes):
    count = rows[0].shape[0]
    n_z, _, width, hidden = up_down.shape
    whole = pl.BlockSpec((count, width), lambda i: (0, 0))
    weight = pl.BlockSpec((1, 2, width, hidden), lambda i: (i, 0, 0, 0))
    kept = pl.BlockSpec((1, count, hidden), lambda i: (i, 0, 0))
    kept_out = 1 if kept_in else 2
    return pl.pallas_call(
        kernel,
        grid=(n_z,),
        out_shape=(jax.ShapeDtypeStruct((count, width), out_type),) * wholes
        + (jax.ShapeDtypeStruct((n_z, count, hidden), bf16),) * kept_out,
        in_specs=[whole] * len(rows) + [kept] * len(kept_in) + [weight],
        out_specs=(whole,) * wholes + (kept,) * kept_out,
        scratch_shapes=[pltpu.VMEM((count, width), f32)] * wholes,
        compiler_params=pltpu.CompilerParams(vmem_limit_bytes=VMEM),
        cost_estimate=effort(12 * count * width * hidden * n_z * wholes),
        name=name,
    )(*rows, *kept_in, up_down)


def expert_grad_kernel(b_ref, b_other, dy_ref, dy_other, du_ref, du_other, g_ref, g_other, out_ref):
    grad_up = dot_tn(b_ref[...], du_ref[0]) + dot_tn(b_other[...], du_other[0])
    out_ref[0, 0] = grad_up.astype(bf16)
    grad_down = dot_tn(dy_ref[...], g_ref[0]) + dot_tn(dy_other[...], g_other[0])
    out_ref[0, 1] = grad_down.astype(bf16)


def expert_grad(rows, kept):
    width = rows[2].shape[1]
    n_z, _, hidden = kept[0].shape
    return pl.pallas_call(
        expert_grad_kernel,
        grid=(n_z,),
        out_shape=jax.ShapeDtypeStruct((n_z, 2, width, hidden), bf16),
        in_specs=[pl.BlockSpec((v.shape[0], width), lambda i: (0, 0)) for v in rows]
        + [pl.BlockSpec((1,) + v.shape[1:], lambda i: (i, 0, 0)) for v in kept],
        out_specs=pl.BlockSpec((1, 2, width, hidden), lambda i: (i, 0, 0, 0)),
        compiler_params=pltpu.CompilerParams(vmem_limit_bytes=VMEM),
        cost_estimate=effort(5 * 2 * sum(v.shape[0] for v in rows) * width * hidden * n_z),
        name="expert_grad",
    )(*rows, *kept)


def weight_grad_kernel(a_ref, q_ref, kv_ref, out_grad_ref, context_ref, small_ref, out_ref):
    part = q_ref.shape[1]
    cut = part + kv_ref.shape[1]
    wide = cut + small_ref.shape[1]
    out_ref[:, :part] = dot_tn(a_ref[...], q_ref[...]).astype(bf16)
    out_ref[:, part:cut] = dot_tn(a_ref[...], kv_ref[...]).astype(bf16)
    out_ref[:, cut:wide] = small_ref[...].astype(bf16)
    out_ref[:, wide:] = dot_tn(out_grad_ref[...], context_ref[...]).astype(bf16)


def weight_grad(a, grad_q, grad_kv, out_grad, context, small):
    width = a.shape[1]
    columns = grad_q.shape[1] + grad_kv.shape[1] + small.shape[1] + context.shape[1]
    return pl.pallas_call(
        weight_grad_kernel,
        out_shape=jax.ShapeDtypeStruct((width, columns), bf16),
        in_specs=vmem_specs(6),
        out_specs=vmem_specs(1)[0],
        compiler_params=pltpu.CompilerParams(vmem_limit_bytes=VMEM),
        cost_estimate=effort(4 * 2 * a.shape[0] * width * columns),
        name="weight_grad",
    )(a, grad_q, grad_kv, out_grad, context, small)


def local(
    tokens,
    cotangent,
    gain_attn,
    query_w,
    key_w,
    value_w,
    output_w,
    rel_table,
    rel_bucket,
    gain_ffn,
    router_w,
    routes,
    expert_in,
    expert_out,
):
    seq_count, local_len, width = tokens.shape
    tok = seq_count * local_len
    n_dp, n_seq = lax.axis_size("dp"), lax.axis_size("seq")
    head_count = rel_table.shape[1]
    inner = query_w.shape[1]
    size = inner // head_count
    n_z = math.gcd(head_count, n_seq)
    n_y = n_seq // n_z
    heads = head_count // n_z
    part = heads * size
    experts = router_w.shape[1]
    capacity = 2 * tok // experts
    table_rows = rel_table.shape[0]
    buckets = table_rows * n_seq
    w_rows = query_w.shape[0]
    dims = (n_z, n_y, local_len)
    dp, seq = lax.axis_index("dp"), lax.axis_index("seq")
    z, y = seq // n_y, seq % n_y
    dp_bits, y_bits, z_bits = bits_of(n_dp), bits_of(n_y), bits_of(n_z)

    def swap_z(value, k):
        return swap(value, "seq", k * n_y) if k else value

    def swap_y(value, k):
        return swap(value, "seq", k) if k else value

    def swap_dp(value, k):
        return swap(value, "dp", k) if k else value

    extra = jnp.concatenate([gain_attn[:, None], gain_ffn[:, None], router_w], axis=1)
    extra = jnp.broadcast_to(extra[None], (n_z, w_rows, 2 + experts))
    table_at = part * 3 + 2 + experts
    table = rel_table.reshape(table_rows, n_z, heads).transpose(1, 0, 2)
    table = jnp.pad(table, ((0, 0), (0, w_rows - table_rows), (0, 0)))
    joined = [w.reshape(w_rows, n_z, part).transpose(1, 0, 2) for w in (query_w, key_w, value_w)]
    pack = jnp.concatenate(joined + [extra, table], axis=2)
    packed = -(-pack.shape[2] // 128) * 128
    pack = jnp.pad(pack, ((0, 0), (0, 0), (0, packed - pack.shape[2])))
    by_partner = unxor([pack[j] for j in range(n_z)], z)
    out_t = output_w.T
    by_partner = [jnp.concatenate([v, out_t], axis=1) for v in by_partner]
    gathered = jnp.stack(unxor([swap_z(by_partner[k], k) for k in range(n_z)], z))

    x_own = tokens.reshape(tok, width)
    upward = [(i, i + n_y) for i in range(n_seq - n_y)]
    downward = [(i + n_y, i) for i in range(n_seq - n_y)]
    below, above = [x_own], [x_own]
    for _ in range(n_z - 1):
        below.append(lax.ppermute(below[-1], "seq", upward))
        above.append(lax.ppermute(above[-1], "seq", downward))
    x_parts = [x_own]
    for k in range(1, n_z):
        chosen = x_own
        for j in range(n_z):
            source = j ^ k
            value = below[j - source] if source < j else above[source - j]
            chosen = jnp.where(z == j, value, chosen)
        x_parts.append(chosen)

    for bit in y_bits:
        gathered = grow(gathered, "seq", bit, (y & bit) != 0)
    route_ids = routes.reshape(tok)
    choose = route_ids[:, None] == jnp.arange(experts, dtype=jnp.int32)[None, :]
    choose_f = choose.astype(f32)
    before = jnp.arange(tok)[:, None] > jnp.arange(tok)[None, :]
    earlier = dot_nn(before.astype(bf16), choose.astype(bf16))
    slot = jnp.sum(earlier * choose_f, axis=1).astype(jnp.int32)
    place = (route_ids ^ dp) * capacity + slot
    place_hot = jnp.arange(experts * capacity, dtype=jnp.int32)[:, None] == place[None, :]
    place_b = place_hot.astype(bf16)

    def to_experts(values):
        sent = dot_nn(place_b, values).astype(bf16).reshape(experts, capacity, -1)
        return [swap_dp(sent[k], k) for k in range(n_dp)]

    def weigh(values, rows):
        gates = rows[:, width : width + 1].astype(f32) + rows[:, width + 1 : width + 2].astype(f32)
        return (values.astype(f32) * gates).astype(bf16)

    def to_others(parts, *others):
        moved = [swap_y(v, k) for k in range(1, n_y) for v in parts]
        return jnp.concatenate([after(v, *others) for v in moved], axis=0)

    def from_experts(total, *others):
        blocks = total.astype(bf16).reshape(n_dp, capacity, width)
        back = [swap_dp(blocks[k], k) for k in range(n_dp)]
        if others:
            back = [after(v, *others) for v in back]
        return dot_tn(place_b, jnp.concatenate(back, axis=0))

    def swap_others(values):
        split = values.reshape(n_y - 1, n_dp * capacity, width)
        return [swap_y(split[k - 1], k) for k in range(1, n_y)]

    upstream_b = cotangent.reshape(tok, width)
    upstream = upstream_b.astype(f32)

    for bit in reversed(dp_bits):
        gathered = grow(gathered, "dp", bit, (dp & bit) != 0)
    n_bits, m_bits = len(y_bits), len(dp_bits)
    order = tuple(reversed(range(m_bits))) + (m_bits + n_bits,)
    order = order + tuple(range(m_bits, m_bits + n_bits)) + (m_bits + n_bits + 1, m_bits + n_bits + 2)
    gathered = gathered.transpose(order).reshape(width, packed + inner)
    out_t = gathered[:, packed:]
    w_qkv = gathered[:, : 3 * part]
    gain_a = gathered[:, 3 * part].astype(f32)
    gain_f = gathered[:, 3 * part + 1].astype(f32)
    w_router = gathered[:, 3 * part + 2 : 3 * part + 2 + experts]
    table = gathered.reshape(n_dp, n_seq, w_rows, packed + inner)[0, :, :table_rows, table_at : table_at + heads]
    table = table.reshape(buckets, heads)

    z_groups = [[j * n_y + i for j in range(n_z)] for i in range(n_y)]
    up_down = jnp.stack([expert_in[0], expert_out[0]])
    x_all, up_down = lax.optimization_barrier((jnp.concatenate(x_parts, axis=0), up_down))
    up_down = lax.all_gather(up_down, "seq", axis=0, axis_index_groups=z_groups)

    x_all = x_all.astype(f32)
    scale_all = lax.rsqrt(jnp.mean(x_all * x_all, axis=-1, keepdims=True) + epsilon)
    normed_all = (x_all * scale_all * gain_a).astype(bf16)
    kv = dot_nn(normed_all, w_qkv[:, part:]).astype(bf16)
    kvs = [swap_y(kv, k) for k in range(n_y)]
    q = dot_nn(normed_all, w_qkv[:, :part]).astype(bf16)
    d_rows = to_experts(after(upstream_b, x_all))
    span = 2 * n_seq * local_len
    bucket_pad = jnp.concatenate([rel_bucket, jnp.full((1,), -1, jnp.int32)])
    bucket_hot = bucket_pad[None, :] == jnp.arange(buckets, dtype=jnp.int32)[:, None]
    table_pad = jnp.pad(table, ((0, 0), (0, 8 - heads)))
    vec = dot_tn(table_pad, bucket_hot.astype(bf16))
    pos = jnp.stack([z, y]).astype(jnp.int32)
    others = tuple(range(1, n_y))
    shape = (dims, seq_count, heads, size)
    before = attn_fwd(*shape, (0,), pos, vec, q, kvs[:1])
    d_rows = [after(v, *before) for v in d_rows]
    d_own = jnp.concatenate(d_rows, axis=0)
    context_parts, context_f = attn_fwd(*shape, others, pos, vec, q, kvs[1:], before)
    d_other = to_others(d_rows, context_parts)
    context_parts = after(context_parts, *d_rows).reshape(n_z, tok, part)
    context = [swap_z(context_parts[k], k) for k in range(n_z)]
    context = jnp.concatenate(unxor(context, z), axis=1)

    inputs = x_own.astype(f32)
    hidden_attn = inputs + dot_nt(context, out_t)
    scale_f = lax.rsqrt(jnp.mean(hidden_attn * hidden_attn, axis=-1, keepdims=True) + epsilon)
    normed_f = (hidden_attn * scale_f * gain_f).astype(bf16)
    logits = dot_nn(normed_f, w_router)
    router_p = jax.nn.softmax(logits, axis=-1)
    gate = jnp.sum(router_p * choose_f, axis=-1)

    gate_high = gate.astype(bf16)
    gate_low = (gate - gate_high.astype(f32)).astype(bf16)
    b_gate = jnp.stack([gate_high, gate_low], axis=1)
    b_gate = jnp.pad(b_gate, ((0, 0), (0, 126)))
    b_rows = to_experts(jnp.concatenate([normed_f, b_gate], axis=1))
    b_own = jnp.concatenate(b_rows, axis=0)
    dy_own = weigh(d_own, b_own)
    b_other = to_others(b_rows)
    dy_other = weigh(d_other, b_other)
    y_other, g_other, slope = expert_call(
        expert_fwd_kernel, "expert_fwd", (b_other,), (), up_down, bf16, 1
    )
    db_other, du_other = expert_call(
        expert_bwd_kernel, "expert_bwd", (dy_other,), (slope,), up_down, bf16, 1
    )
    y_got = swap_others(y_other)
    db_got = swap_others(db_other)
    b_own = after(b_own, db_other, *y_got)
    y_own, db_own, g_own, du_own = expert_call(
        expert_own_kernel, "expert_own", (b_own, dy_own), (), up_down, f32, 2
    )
    y_total = y_own + sum(v.astype(f32) for v in y_got)
    db_total = db_own + sum(v.astype(f32) for v in db_got)
    expert_tok = from_experts(y_total)
    grad_up_down = expert_grad(
        (b_own, b_other, after(dy_own, db_total), dy_other), (du_own, du_other, g_own, g_other)
    )
    grad_normed = from_experts(db_total, grad_up_down)
    grad_up_down = lax.psum_scatter(
        grad_up_down, "seq", scatter_dimension=0, axis_index_groups=z_groups, tiled=True
    )
    grad_up = grad_up_down[:, 0].astype(f32)
    grad_down = grad_up_down[:, 1].astype(f32)

    mixed = (hidden_attn + gate[:, None] * expert_tok).astype(bf16).reshape(tokens.shape)
    grad_gate = jnp.sum(upstream * expert_tok, axis=-1)
    grad_logits = grad_gate[:, None] * router_p * (choose_f - gate[:, None])
    grad_router = lax.dot_general(
        normed_f.astype(f32), grad_logits, (((0,), (0,)), ((), ())), precision=highest
    )
    grad_normed = grad_normed + lax.dot_general(
        grad_logits, w_router.astype(f32), (((1,), (1,)), ((), ())), precision=highest
    )
    scaled = gain_f * grad_normed
    grad_hidden = upstream + scale_f * scaled
    grad_hidden = grad_hidden - hidden_attn * scale_f**3 * jnp.mean(
        scaled * hidden_attn, axis=-1, keepdims=True
    )
    grad_gain_f = jnp.sum(grad_normed * hidden_attn * scale_f, axis=0)
    grad_attn = grad_hidden.astype(bf16)

    grad_ctx = dot_nn(grad_attn, out_t).astype(bf16)
    grad_ctx = unxor([grad_ctx[:, j * part : (j + 1) * part] for j in range(n_z)], z)
    grad_ctx = jnp.concatenate([swap_z(grad_ctx[k], k) for k in range(n_z)], axis=0)
    grad_q, diag, *grad_kvs = attn_bwd(
        *shape, others, pos, vec, q, grad_ctx, context_f, kvs[1:]
    )
    arrived = [swap_y(grad_kvs[k - 1], k) for k in range(1, n_y)]
    grad_q, diag, grad_kv = attn_bwd(
        *shape, (0,), pos, vec, q, grad_ctx, context_f, kvs[:1], (grad_q, diag)
    )
    for value in arrived:
        grad_kv = grad_kv + value.astype(f32)
    grad_kv = grad_kv.astype(bf16)
    grad_qkv = jnp.concatenate([grad_q, grad_kv], axis=1)
    odd, even = list(range(1, n_z, 2)), list(range(0, n_z, 2))

    def take(value, blocks):
        value = value.reshape(n_z, tok, value.shape[1])
        return jnp.concatenate([value[k] for k in blocks], axis=0)

    sent = dot_nt(take(grad_qkv, odd), w_qkv)
    got = swap_z(sent.astype(bf16), 1)
    kept = dot_nt(take(grad_qkv, even), w_qkv)
    grad_gain_a = jnp.sum(sent * take(x_all * scale_all, odd), axis=0)
    grad_gain_a = grad_gain_a + jnp.sum(kept * take(x_all * scale_all, even), axis=0)
    diag = jnp.roll(diag, local_len - 1, axis=1)
    grad_table = lax.dot_general(
        diag, bucket_hot.astype(f32), (((1,), (1,)), ((), ())), precision=highest
    )
    grad_table = grad_table[:heads].T.reshape(1, n_seq, table_rows, heads)
    grad_table = jnp.pad(grad_table, ((0, 0), (0, 0), (0, w_rows - table_rows), (0, 0)))
    grad_table = jnp.broadcast_to(grad_table, (n_dp, n_seq, w_rows, heads)).reshape(width, heads)
    small = [grad_gain_a[:, None], grad_gain_f[:, None], grad_router, grad_table]
    small = jnp.concatenate(small, axis=1)
    small = jnp.pad(small, ((0, 0), (0, packed - 3 * part - small.shape[1])))
    value = weight_grad(normed_all, grad_q, grad_kv, grad_attn, context, small)
    value = value.reshape((2,) * m_bits + (n_z,) + (2,) * n_bits + (w_rows, packed + inner))
    for i, bit in enumerate(dp_bits):
        value = halve(value, m_bits - 1 - i, "dp", bit, (dp & bit) != 0)
    got = after(got, value)
    grad_a = (kept + got.astype(f32)).reshape(n_z // 2, tok, width)
    for bit in bits_of(n_z // 2):
        half = [k for k in range(0, grad_a.shape[0], 2)]
        far = jnp.concatenate([grad_a[k + 1] for k in half]).astype(bf16)
        far = swap_z(far, 2 * bit)
        grad_a = jnp.stack([grad_a[k] for k in half])
        if len(half) > 1:
            grad_a = grad_a + far.astype(f32).reshape(len(half), tok, width)
    for i, bit in enumerate(y_bits):
        value = halve(value, n_bits - i, "seq", bit, (y & bit) != 0)
    value = after(value, grad_a, grad_up_down)
    parts = unxor([value[j] for j in range(n_z)], z)
    summed = unxor([swap_z(parts[k], k) for k in range(n_z)], z)
    grad_query, grad_key, grad_value = (
        jnp.concatenate([v[:, i * part : (i + 1) * part] for v in summed], axis=1).astype(f32)
        for i in range(3)
    )
    total = sum(v[:, 3 * part :].astype(f32) for v in summed)
    grad_gain_attn = total[:, 0]
    grad_gain_ffn = total[:, 1]
    grad_router = total[:, 2 : 2 + experts]
    grad_output = total[:, packed - 3 * part :].T
    grad_table = jnp.concatenate(
        [v[:table_rows, table_at : table_at + heads] for v in summed], axis=1
    ).astype(f32)

    far, grad_output = lax.optimization_barrier((far, grad_output))
    grad_a = grad_a[0] + far.astype(f32)
    scale_a = scale_all[:tok]
    scaled_a = gain_a * grad_a
    grad_x = grad_hidden + scale_a * scaled_a
    grad_x = grad_x - inputs * scale_a**3 * jnp.mean(scaled_a * inputs, axis=-1, keepdims=True)
    grad_tokens = grad_x.reshape(tokens.shape)

    return (
        mixed,
        grad_tokens,
        grad_gain_attn,
        grad_query,
        grad_key,
        grad_value,
        grad_output,
        grad_table,
        grad_gain_ffn,
        grad_router,
        grad_up,
        grad_down,
    )


def solution(mesh):
    vector = P(("dp", "seq"))
    matrix = P(("dp", "seq"), None)
    rows = P("dp", "seq", None)
    expert = P("dp", None, "seq")
    last = P(None, ("dp", "seq"))
    table = P("seq", None)
    return jax.shard_map(
        local,
        mesh=mesh,
        in_specs=(
            rows,
            rows,
            vector,
            matrix,
            matrix,
            matrix,
            last,
            table,
            P(),
            vector,
            matrix,
            P("dp", "seq", None, None),
            expert,
            expert,
        ),
        out_specs=(
            rows,
            rows,
            vector,
            matrix,
            matrix,
            matrix,
            last,
            table,
            vector,
            matrix,
            expert,
            expert,
        ),
        check_vma=False,
    )
```
